512 devices in a mesh: dp: 32 (over x, y, core), fsdp: 16 (over z).
Axes of the slice: x: 4, y: 4, z: 16, core: 2. Of those that a mesh axis runs over, the one named last changes fastest.
Arguments:
- layer_input: bfloat16 [131072, 5120], P(('dp', 'fsdp')), may hold values from -6 to 6
- queries: bfloat16 [131072, 2048], P(('dp', 'fsdp')), may hold values from -140 to 140
- key_states: bfloat16 [131072, 256], P(('dp', 'fsdp')), may hold values from -4.25 to 4.25
- upstream: bfloat16 [131072, 2048], P(('dp', 'fsdp')), may hold values from -6 to 6
- advantage: float32 [131072], P(('dp', 'fsdp')), may hold values from -4 to 4
- value_weight: bfloat16 [5120, 256], P('fsdp'), may hold values from -0.078125 to 0.078125
- row_sample: int32 [131072], P(('dp', 'fsdp')), may hold values from -1 to 255, as said below
- row_rank: int32 [131072], P(('dp', 'fsdp')), may hold values from 0 to 31, as said below
- row_pack: int32 [131072], P(('dp', 'fsdp')), may hold values from 0 to 127, as said below
Outputs:
- key_grad: bfloat16 [65536, 256], P(('dp', 'fsdp'))
- weight_grad: float32 [5120, 256], P('fsdp')
The draws below stay inside these ranges and needn't reach their ends.
Inputs may be any that keep to these rules, and one draw needn't show every extreme that they name: `row_sample`: -1 marks an empty slot; otherwise the answer's number, unique among the devices of one fsdp index; an answer's rows are consecutive on one device, in order, and number at most 16. `row_rank`: the training device has the same fsdp index; all rows of an answer share it; one device sends another at most one answer; 0 on empty slots. `row_pack`: rows that go to one device take different places, an answer's rows consecutive places in order; a device receives at most 128 rows, and some device exactly 128; 0 on empty slots.
All inputs are finite; a program needn't handle non-finite values.
Results may differ from the reference program's by a relative error of at most 0.028.
Values may be sent and summed in bfloat16 or wider, within the bound.
A program may use at most 64 MiB of HBM per device.

```python
import jax
import jax.numpy as jnp
from jax import lax

D = 5120
HEADS = 32
KV_HEADS = 4
HEAD_DIM = 64
UNITS = 8
BAL = 128
OWN = 256
MAXLEN = 16
TOKENS = 131072
PACKED = 65536
N_DP = 32
N_FSDP = 16
DEVICES = 512


def column_layout(key):
    unit_total = N_DP * UNITS
    split_keys = jax.random.split(key, 4)
    most_skew = min(UNITS, N_DP - UNITS)
    pair_skew = jax.random.randint(split_keys[0], (N_DP // 2,), 0, most_skew + 1)
    pair_skew = pair_skew.at[0].set(most_skew)
    counts = jnp.stack([UNITS + pair_skew, UNITS - pair_skew], axis=1).reshape(N_DP)
    counts = counts[jax.random.permutation(split_keys[1], N_DP)]
    unit_ends = jnp.cumsum(counts)
    starts = unit_ends - counts
    unit_index = jnp.arange(unit_total, dtype=jnp.int32)
    unit_owner = jnp.sum((unit_ends[None, :] <= unit_index[:, None]).astype(jnp.int32), axis=1)
    unit_rank = unit_index % N_DP
    unit_length = jax.random.randint(split_keys[2], (unit_total,), max(1, MAXLEN // 4), MAXLEN + 1)
    full_rank = jax.random.randint(split_keys[3], (), 0, N_DP)
    unit_length = jnp.where(unit_rank == full_rank, MAXLEN, unit_length)
    running_len = jnp.cumsum(unit_length) - unit_length
    own_off = running_len - running_len[starts[unit_owner]]
    by_rank = unit_length.reshape(UNITS, N_DP)
    pack_off = (jnp.cumsum(by_rank, axis=0) - by_rank).reshape(unit_total)
    row_index = jnp.arange(OWN, dtype=jnp.int32)[None, :, None]
    member = (unit_owner[None, None, :] == jnp.arange(N_DP, dtype=jnp.int32)[:, None, None]) & (own_off[None, None, :] <= row_index) & (row_index < (own_off + unit_length)[None, None, :])
    member_int = member.astype(jnp.int32)
    is_live = jnp.sum(member_int, axis=2)
    inside = row_index - own_off[None, None, :]
    sample = jnp.sum(member_int * unit_index[None, None, :], axis=2) - (1 - is_live)
    dest_rank = jnp.sum(member_int * unit_rank[None, None, :], axis=2)
    in_sample = jnp.sum(member_int * inside, axis=2)
    pack_place = jnp.sum(member_int * (pack_off[None, None, :] + inside), axis=2)
    return (sample.astype(jnp.int32), dest_rank.astype(jnp.int32), in_sample.astype(jnp.int32), pack_place.astype(jnp.int32))


def unit_layout(key):
    column_keys = jax.random.split(jax.random.fold_in(key, 202), N_FSDP)
    layouts = lax.map(column_layout, column_keys)
    return tuple((jnp.transpose(layout_part, (1, 0, 2)).reshape(TOKENS) for layout_part in layouts))


def shared_base(key):
    return jnp.clip(jax.random.normal(jax.random.fold_in(key, 101), (TOKENS, KV_HEADS * HEAD_DIM), jnp.float32), -4.0, 4.0)


def draw_row_sample(key, part):
    layout = unit_layout(key)
    return layout[0]


def draw_row_rank(key, part):
    layout = unit_layout(key)
    return layout[1]


def draw_row_pack(key, part):
    layout = unit_layout(key)
    return layout[3]


def draw_key_states(key, part):
    base = shared_base(key)
    key = jax.random.fold_in(key, 7)
    return base.astype(jnp.bfloat16)


def draw_queries(key, part):
    key = jax.random.fold_in(key, 5)
    plain = jnp.clip(jax.random.normal(key, (TOKENS, HEADS * HEAD_DIM), jnp.float32), -4.0, 4.0)
    return plain.astype(jnp.bfloat16)


def shard_levels(stream_key, extent, pieces, least, top_value):
    factor_of, own = 1.0, jax.random.fold_in(stream_key, 6)
    for dim, blocks in pieces:
        draws = jnp.exp(jax.random.uniform(jax.random.fold_in(own, dim), (blocks,), jnp.float32, least / len(pieces), top_value / len(pieces)))
        factor_of = factor_of * jnp.repeat(draws, extent[dim] // blocks).reshape([-1 if axis == dim else 1 for axis in range(len(extent))])
    return factor_of


def scatter_about(key, shape, scale, most, pieces=(), held_as=jnp.bfloat16):
    entries = jax.random.normal(key, shape, jnp.float32) * scale
    if len(pieces) > 0:
        entries = shard_levels(key, shape, pieces, -0.22, 0.18) * entries
    return jnp.clip(entries, min=-most, max=most).astype(held_as)


def setup_inputs(seed: int = 0) -> dict:
    key_list = jax.random.split(jax.random.key(seed), 10)
    layer_input = scatter_about(key_list[0], (TOKENS, D), 1.0, 6.0, ((0, 512),))
    queries = draw_queries(jax.random.fold_in(key_list[9], 71), 0)
    key_states = draw_key_states(jax.random.fold_in(key_list[9], 71), 0)
    upstream = scatter_about(key_list[3], (TOKENS, HEADS * HEAD_DIM), 1.0, 6.0, ((0, 512),))
    advantage = scatter_about(key_list[4], (TOKENS,), 1.0, 4.0, ((0, 512),), jnp.float32)
    value_weight = scatter_about(key_list[5], (D, KV_HEADS * HEAD_DIM), D ** -0.5, 0.078125, ((0, 16),))
    row_sample = draw_row_sample(jax.random.fold_in(key_list[9], 71), 0)
    row_rank = draw_row_rank(jax.random.fold_in(key_list[9], 71), 0)
    row_pack = draw_row_pack(jax.random.fold_in(key_list[9], 71), 0)
    return dict(layer_input=layer_input, queries=queries, key_states=key_states, upstream=upstream, advantage=advantage, value_weight=value_weight, row_sample=row_sample, row_rank=row_rank, row_pack=row_pack)


def attend_block(queries, key_states, values, grad_out, samples):
    length = queries.shape[0]
    per_group = HEADS // KV_HEADS
    att_scale = HEAD_DIM ** -0.5
    query_heads = queries.astype(jnp.float32).reshape(length, KV_HEADS, per_group, HEAD_DIM)
    key_heads = key_states.astype(jnp.float32).reshape(length, KV_HEADS, HEAD_DIM)
    value_heads = values.astype(jnp.float32).reshape(length, KV_HEADS, HEAD_DIM)
    grad_heads = grad_out.astype(jnp.float32).reshape(length, KV_HEADS, per_group, HEAD_DIM)
    places = jnp.arange(length)
    allowed = (samples[:, None] == samples[None, :]) & (places[:, None] >= places[None, :])
    scores = jnp.einsum("tkgd,skd->kgts", query_heads, key_heads) * att_scale
    scores = jnp.where(allowed[None, None], scores, -jnp.inf)
    row_max = jnp.max(scores, axis=-1, keepdims=True)
    exponent = jnp.exp(scores - row_max)
    soft_weights = exponent / jnp.sum(exponent, axis=-1, keepdims=True)
    rounded = lax.optimization_barrier(soft_weights.astype(jnp.bfloat16)).astype(jnp.float32)
    outputs = jnp.einsum("kgts,skd->tkgd", rounded, value_heads)
    value_grad = jnp.einsum("kgts,tkgd->skd", rounded, grad_heads)
    prob_grad = jnp.einsum("tkgd,skd->kgts", grad_heads, value_heads)
    row_delta = jnp.einsum("tkgd,tkgd->kgt", grad_heads, outputs)
    score_grad = soft_weights * (prob_grad - row_delta[..., None]) * att_scale
    score_grad = lax.optimization_barrier(score_grad.astype(jnp.bfloat16)).astype(jnp.float32)
    key_grad = jnp.einsum("kgts,tkgd->skd", score_grad, query_heads)
    return value_grad.reshape(length, -1).astype(jnp.bfloat16), key_grad.reshape(length, -1).astype(jnp.bfloat16)


def sample_counts(block_samples):
    same_sample = block_samples[:, None] == block_samples[None, :]
    return jnp.sum(same_sample, axis=1).astype(jnp.float32)


def reference(layer_input, queries, key_states, upstream, advantage, value_weight, row_sample, row_rank, row_pack):
    kv_width = KV_HEADS * HEAD_DIM
    values = jnp.dot(layer_input, value_weight, preferred_element_type=jnp.float32).astype(jnp.bfloat16)
    is_live = row_sample >= 0
    counts = lax.map(sample_counts, row_sample.reshape(DEVICES, OWN)).reshape(TOKENS)
    factor = jnp.where(is_live, advantage / counts, 0.0)
    grad_out = (factor[:, None] * upstream.astype(jnp.float32)).astype(jnp.bfloat16)
    blocks = (queries.reshape(DEVICES, OWN, -1), key_states.reshape(DEVICES, OWN, -1), values.reshape(DEVICES, OWN, -1), grad_out.reshape(DEVICES, OWN, -1), row_sample.reshape(DEVICES, OWN))

    def attend_one(packed_in):
        return attend_block(packed_in[0], packed_in[1], packed_in[2], packed_in[3], packed_in[4])

    value_grad, key_rows = lax.map(attend_one, blocks)

    def add_term(running, paired):
        input_block, grad_block = paired
        device_term = jnp.dot(input_block.T, grad_block, preferred_element_type=jnp.float32)
        device_term = lax.optimization_barrier(device_term.astype(jnp.bfloat16)).astype(jnp.float32)
        return running + device_term, None

    weight_grad = lax.scan(add_term, jnp.zeros((D, kv_width), jnp.float32), (layer_input.reshape(DEVICES, OWN, D), value_grad))[0]
    block_index = jnp.arange(TOKENS, dtype=jnp.int32) // OWN
    fsdp_index = block_index % N_FSDP
    target = (row_rank * N_FSDP + fsdp_index) * BAL + row_pack
    target = jnp.where(is_live, target, PACKED).astype(jnp.int32)
    key_grad = jnp.zeros((PACKED, kv_width), jnp.bfloat16).at[target].set(key_rows.reshape(TOKENS, kv_width), mode="drop")
    return key_grad, weight_grad
```

```python
import functools

import jax
import jax.numpy as jnp
from jax import lax
from jax.experimental import pallas as pl
from jax.experimental.pallas import tpu as pltpu
from jax.sharding import PartitionSpec as P

NX, NY, CORES = 4, 4, 2
KV_HEADS = 4
HEAD_DIM = 64
BAL = 128
MAXLEN = 16
LANES = 128
NH = NY // 2
MESH = pl.DeviceIdType.MESH
BF16, F32 = jnp.bfloat16, jnp.float32
NEG = -1e30
BLOCKS = ((0, 0, 128), (128, 112, 144))
NT = (((1,), (1,)), ((), ()))
TN = (((0,), (0,)), ((), ()))


def spread_heads(source, kb, scale):
    rows = source.shape[0]
    lane = lax.broadcasted_iota(jnp.int32, (rows, LANES), 1)
    zero = jnp.zeros((rows, LANES), BF16)
    for pair in range(2):
        tile = source[:, pair * LANES : (pair + 1) * LANES].astype(F32) * scale
        swapped = pltpu.roll(tile, HEAD_DIM, 1)
        for odd in range(2):
            g = 2 * pair + odd
            low = jnp.where(lane < HEAD_DIM, tile if odd == 0 else swapped, 0.0).astype(BF16)
            high = jnp.where(lane >= HEAD_DIM, tile if odd == 1 else swapped, 0.0).astype(BF16)
            for r in range(4):
                kb[g, r, :, pl.ds((r // 2) * LANES, LANES)] = low if r % 2 == 0 else high
                kb[g, r, :, pl.ds((1 - r // 2) * LANES, LANES)] = zero


def head_sum(parts, tiles, rows):
    even = jnp.concatenate([parts[i] for i in (0, 2, 4, 6)], axis=1)
    odd = jnp.concatenate([parts[i] for i in (1, 3, 5, 7)], axis=1)
    both = jnp.dot(
        jnp.concatenate([even, odd], axis=0),
        jnp.concatenate(tiles, axis=0),
        preferred_element_type=F32,
    )
    return both[:rows] + pltpu.roll(both[rows:], HEAD_DIM, 1)


def put_rows(acc, g, block, w):
    if block == 0:
        acc[g, 0:128, :] = w
    else:
        acc[g, 112:128, :] = acc[g, 112:128, :] + w[:16]
        acc[g, 128:256, :] = w[16:]


def join_heads(acc):
    rows = acc.shape[1]
    lane = lax.broadcasted_iota(jnp.int32, (rows, LANES), 1)
    tiles = []
    for pair in range(2):
        tiles.append(
            jnp.where(lane < HEAD_DIM, acc[2 * pair], pltpu.roll(acc[2 * pair + 1], HEAD_DIM, 1))
        )
    return jnp.concatenate(tiles, axis=1).astype(BF16)


def kernel(
    nz,
    x_hbm,
    q_hbm,
    k_hbm,
    u_hbm,
    w_hbm,
    adv_ref,
    samp_ref,
    rank_ref,
    pack_ref,
    kg_ref,
    wg_ref,
    qv,
    uv,
    kv,
    xv,
    wf,
    kb,
    p0,
    p1,
    bias0,
    bias1,
    frow,
    acc,
    vg,
    vg_sib,
    tacc,
    tb,
    ra,
    rb,
    sa,
    sb,
    qa,
    qb,
    fb,
    zb,
    gb,
    vp,
    vp_sib,
    s1h,
    ks,
    kr,
    ps,
    pr,
    loc,
    xs_sem,
    vg_sem,
    vp_sem,
    wz_send,
    wz_recv,
    ws_send,
    ws_recv,
    wl_send,
    wl_recv,
    p1_send,
    p1_recv,
    p2_send,
    p2_recv,
    z_send,
    z_recv,
    g_send,
    g_recv,
    ps_sem,
    kk_sem,
):
    ndp = NX * NY * CORES
    half = nz // 2
    n_all = half // NH
    ni = n_all // 2
    own = q_hbm.shape[0]
    width = x_hbm.shape[1] // 2
    shard = w_hbm.shape[0]
    piece = shard // NX
    me = lax.axis_index("dp")
    z = lax.axis_index("fsdp")
    core = me % CORES
    x = me // CORES // NY
    y = me // CORES % NY
    h, ch = y // 2, y % 2
    is_src = jnp.logical_and(z // half == core, z % NH == h)
    own_n = z % half // NH
    sib = me + 1 - 2 * core

    def at(dx, dy):
        return ((dx * NY + dy) * CORES + core, z)

    def xrows(dx):
        return pl.ds(pl.multiple_of(dx * piece, 16), piece)

    def remote(src, dst, send, recv, device):
        return pltpu.make_async_remote_copy(
            src_ref=src,
            dst_ref=dst,
            send_sem=send,
            recv_sem=recv,
            device_id=device,
            device_id_type=MESH,
        )

    kcopy = pltpu.make_async_copy(k_hbm, kv, loc.at[0])
    qcopy = pltpu.make_async_copy(q_hbm, qv, loc.at[1])
    ucopy = pltpu.make_async_copy(u_hbm, uv, loc.at[2])
    xcopy = pltpu.make_async_copy(
        x_hbm.at[:, pl.ds(pl.multiple_of(core * width, LANES), width)], xv.at[0], loc.at[3]
    )
    w_piece = w_hbm.at[xrows(x), pl.ds(pl.multiple_of(ch * LANES, LANES), LANES)]
    wcopy = pltpu.make_async_copy(w_piece, wf.at[own_n, h, ch, xrows(x)], loc.at[4])
    kcopy.start()
    qcopy.start()
    ucopy.start()
    xcopy.start()

    @pl.when(is_src)
    def _():
        wcopy.start()

    barrier = pltpu.get_barrier_semaphore()

    def greet_dp(s, carry):
        pl.semaphore_signal(barrier, inc=1, device_id=((me + s) % ndp, z), device_id_type=MESH)
        return carry

    def greet_z(s, carry):
        pl.semaphore_signal(barrier, inc=1, device_id=(me, (z + s) % nz), device_id_type=MESH)
        return carry

    lax.fori_loop(1, ndp, greet_dp, 0)
    lax.fori_loop(1, nz, greet_z, 0)

    samp = samp_ref[...].astype(F32)
    col = jnp.transpose(jnp.broadcast_to(samp, (LANES, own)))
    s_at = lax.broadcasted_iota(jnp.int32, (own, LANES), 0)
    live = samp >= 0
    slots = []
    for b, (t0, k0, nk) in enumerate(BLOCKS):
        same = col == samp[:, t0 : t0 + LANES]
        t_at = lax.broadcasted_iota(jnp.int32, (own, LANES), 1) + t0
        count = jnp.sum(jnp.where(same, 1.0, 0.0), axis=0, keepdims=True)
        slots.append(
            jnp.sum(jnp.where(jnp.logical_and(same, s_at < t_at), 1.0, 0.0), axis=0, keepdims=True)
        )
        bias = jnp.where(jnp.logical_and(same, s_at <= t_at), 0.0, NEG)
        (bias0, bias1)[b][...] = bias[k0 : k0 + nk]
        frow[b] = jnp.where(
            live[:, t0 : t0 + LANES], adv_ref[:, t0 : t0 + LANES] / count, 0.0
        )
    slot = jnp.concatenate(slots, axis=1)
    rank = rank_ref[...]
    rel = jnp.where(rank >= me, rank - me, rank - me + ndp)
    target = jnp.where(live, rel.astype(F32) * MAXLEN + slot, -1.0).astype(jnp.int32)
    n_slots = ndp * MAXLEN
    s1h[...] = jnp.where(
        lax.broadcasted_iota(jnp.int32, (n_slots, own), 0) == target, 1.0, 0.0
    ).astype(BF16)
    first = jnp.where(jnp.logical_and(live, slot == 0), rel, -1)
    pack = pack_ref[...].astype(F32)
    hit = lax.broadcasted_iota(jnp.int32, (ndp, 8, own), 0) == first[None]
    begin = jnp.sum(jnp.where(hit, pack[None], 0.0), axis=2, keepdims=True)
    ps[...] = jnp.broadcast_to(begin, (ndp, 8, LANES))
    pr[0] = ps[0]

    kcopy.wait()
    spread_heads(kv, kb, HEAD_DIM**-0.5)

    pl.semaphore_wait(barrier, ndp - 1 + nz - 1)

    @pl.when(is_src)
    def _():
        def send(s, carry):
            remote(
                w_piece,
                wf.at[own_n, h, ch, xrows(x)],
                wz_send.at[s - 1],
                wz_recv.at[own_n],
                (me, (z + s) % nz),
            ).start()
            return carry

        lax.fori_loop(1, nz, send, 0)

    x_sib = remote(
        x_hbm.at[:, pl.ds(pl.multiple_of((1 - core) * width, LANES), width)],
        xv.at[1],
        xs_sem.at[0],
        xs_sem.at[1],
        (sib, z),
    )
    x_sib.start()

    def send_begin(s, carry):
        remote(ps.at[s], pr.at[s], ps_sem.at[0], ps_sem.at[1], ((me + s) % ndp, z)).start()
        return carry

    lax.fori_loop(1, ndp, send_begin, 0)

    qcopy.wait()
    ucopy.wait()

    def forward(g, carry):
        at_lane = g * 512
        for b, (t0, k0, nk) in enumerate(BLOCKS):
            keys = kb[g, :, k0 : k0 + nk, :].reshape(4 * nk, 256)
            bias = (bias0, bias1)[b][...]
            parts = []
            for part in range(2):
                lanes = pl.ds(pl.multiple_of(at_lane + part * 256, 256), 256)
                s = lax.dot_general(
                    keys, qv[t0 : t0 + LANES, lanes], NT, preferred_element_type=F32
                )
                s = s.reshape(4, nk, LANES) + bias[None]
                e = jnp.exp(s - jnp.max(s, axis=1, keepdims=True))
                soft = e * (1.0 / jnp.sum(e, axis=1, keepdims=True))
                (p0, p1)[b][g * 2 + part] = soft
                scaled = (soft * frow[b][None]).astype(BF16)
                parts += [scaled[r] for r in range(4)]
            tiles = [
                uv[t0 : t0 + LANES, pl.ds(pl.multiple_of(at_lane + i * LANES, LANES), LANES)]
                for i in range(4)
            ]
            put_rows(acc, g, b, head_sum(parts, tiles, nk))
        return carry

    lax.fori_loop(0, 2, forward, 0)

    for n in range(n_all):
        @pl.when(jnp.logical_not(jnp.logical_and(is_src, own_n == n)))
        def _():
            dst = wf.at[n, h, ch, xrows(x)]
            remote(dst, dst, wz_send.at[0], wz_recv.at[n], (me, (z + 1) % nz)).wait_recv()

    @pl.when(is_src)
    def _():
        wcopy.wait()

    mine_a = wf.at[0:ni, h, ch, xrows(x)]
    mine_b = wf.at[ni:n_all, h, ch, xrows(x)]
    w_small = []
    for s in range(1, NY):
        i = s - 1
        to, src = (y + s) % NY, (y + NY - s) % NY
        c = remote(mine_a, mine_a, ws_send.at[0, i], ws_recv.at[0, i], at(x, to))
        c.start()
        dst = wf.at[0:ni, src // 2, src % 2, xrows(x)]
        w_small.append((c, remote(dst, dst, ws_send.at[0, i], ws_recv.at[0, i], at(x, src))))
    for s in range(1, NX):
        i = s - 1
        to, src = (x + s) % NX, (x + NX - s) % NX
        c = remote(mine_b, mine_b, ws_send.at[1, i], ws_recv.at[1, i], at(to, y))
        c.start()
        dst = wf.at[ni:n_all, h, ch, xrows(src)]
        w_small.append((c, remote(dst, dst, ws_send.at[1, i], ws_recv.at[1, i], at(src, y))))

    lax.fori_loop(2, 4, forward, 0)
    vg[...] = join_heads(acc)
    vg_sib_copy = remote(vg, vg_sib, vg_sem.at[0], vg_sem.at[1], (sib, z))
    vg_sib_copy.start()

    for c, r in w_small:
        r.wait_recv()
    w_large = []
    line_a = wf.at[0:ni, :, :, xrows(x)]
    line_b = wf.at[ni:n_all, h, ch]
    for s in range(1, NX):
        i = s - 1
        to, src = (x + s) % NX, (x + NX - s) % NX
        c = remote(line_a, line_a, wl_send.at[0, i], wl_recv.at[0, i], at(to, y))
        c.start()
        dst = wf.at[0:ni, :, :, xrows(src)]
        w_large.append((c, remote(dst, dst, wl_send.at[0, i], wl_recv.at[0, i], at(src, y))))
    for s in range(1, NY):
        i = s - 1
        to, src = (y + s) % NY, (y + NY - s) % NY
        c = remote(line_b, line_b, wl_send.at[1, i], wl_recv.at[1, i], at(x, to))
        c.start()
        dst = wf.at[ni:n_all, src // 2, src % 2]
        w_large.append((c, remote(dst, dst, wl_send.at[1, i], wl_recv.at[1, i], at(x, src))))

    chunk = NH * shard
    xcopy.wait()

    def term_own(n, carry):
        lanes = pl.ds(pl.multiple_of(n * chunk, LANES), chunk)
        tacc[n] = lax.dot_general(xv[0, :, lanes], vg[...], TN, preferred_element_type=F32)
        return carry

    lax.fori_loop(0, n_all, term_own, 0)
    x_sib.wait_recv()
    vg_sib_copy.wait_recv()

    def term_sib(n, carry):
        lanes = pl.ds(pl.multiple_of(n * chunk, LANES), chunk)
        total = tacc[n] + lax.dot_general(
            xv[1, :, lanes], vg_sib[...], TN, preferred_element_type=F32
        )
        total = total.astype(BF16)
        for c in range(2):
            tb[n, :, c] = total[:, c * LANES : (c + 1) * LANES].reshape(NH, shard, LANES)
        return carry

    first_sum = []
    lax.fori_loop(0, ni, term_sib, 0)
    for s in range(1, NX):
        i = s - 1
        to = (x + s) % NX
        c = remote(
            tb.at[0:ni, :, :, xrows(to)], ra.at[i], p1_send.at[0, i], p1_recv.at[0, i], at(to, y)
        )
        c.start()
        first_sum.append(c)
    lax.fori_loop(ni, n_all, term_sib, 0)
    for s in range(1, NY):
        i = s - 1
        to = (y + s) % NY
        c = remote(
            tb.at[ni:n_all, to // 2, to % 2],
            rb.at[i],
            p1_send.at[1, i],
            p1_recv.at[1, i],
            at(x, to),
        )
        c.start()
        first_sum.append(c)

    for c, r in w_large:
        r.wait_recv()

    def value_part(n, carry):
        lanes = pl.ds(pl.multiple_of(n * chunk, LANES), chunk)
        weights = jnp.concatenate(
            [wf[n, :, c].reshape(chunk, LANES) for c in range(2)], axis=1
        )
        rows = xv[:, :, lanes].reshape(2 * own, chunk)
        part = jnp.dot(rows, weights, preferred_element_type=F32).reshape(2, own, 256)
        vp[...] = jnp.where(n == 0, part, vp[...] + part)
        return carry

    vp[...] = jnp.zeros(vp.shape, F32)
    lax.fori_loop(0, n_all, value_part, 0)
    vp_copy = remote(vp.at[1], vp_sib, vp_sem.at[0], vp_sem.at[1], (sib, z))
    vp_copy.start()
    vp_copy.wait_recv()
    vg_sib_copy.wait_send()
    kv[...] = (vp[0] + vp_sib[...]).astype(BF16)
    spread_heads(kv, kb, 1.0)

    def backward(g, carry):
        at_lane = g * 512
        for b, (t0, k0, nk) in enumerate(BLOCKS):
            vals = kb[g, :, k0 : k0 + nk, :].reshape(4 * nk, 256)
            parts = []
            for part in range(2):
                lanes = pl.ds(pl.multiple_of(at_lane + part * 256, 256), 256)
                d = lax.dot_general(
                    vals, uv[t0 : t0 + LANES, lanes], NT, preferred_element_type=F32
                )
                d = d.reshape(4, nk, LANES)
                soft = (p0, p1)[b][g * 2 + part]
                delta = jnp.sum(soft * d, axis=1, keepdims=True)
                grad = soft * (d - delta) * (frow[b] * HEAD_DIM**-0.5)[None]
                grad = grad.astype(BF16)
                parts += [grad[r] for r in range(4)]
            tiles = [
                qv[t0 : t0 + LANES, pl.ds(pl.multiple_of(at_lane + i * LANES, LANES), LANES)]
                for i in range(4)
            ]
            put_rows(acc, g, b, head_sum(parts, tiles, nk))
        return carry

    lax.fori_loop(0, 4, backward, 0)
    rows = jnp.dot(s1h[...], join_heads(acc), preferred_element_type=F32).astype(BF16)
    ks[...] = rows.reshape(ndp, MAXLEN, 256)
    kr[0] = ks[0]

    def send_rows(s, carry):
        remote(ks.at[s], kr.at[s], kk_sem.at[0], kk_sem.at[1], ((me + s) % ndp, z)).start()
        return carry

    lax.fori_loop(1, ndp, send_rows, 0)

    for c in first_sum[: NX - 1]:
        c.wait_recv()
    total = tb[0:ni, :, :, xrows(x)].astype(F32)
    for i in range(NX - 1):
        total = total + ra[i].astype(F32)
    sa[...] = total.astype(BF16)
    second_sum = []
    for s in range(1, NY):
        i = s - 1
        to = (y + s) % NY
        c = remote(
            sa.at[:, to // 2, to % 2], qa.at[i], p2_send.at[0, i], p2_recv.at[0, i], at(x, to)
        )
        c.start()
        second_sum.append(c)
    for c in first_sum[NX - 1 :]:
        c.wait_recv()
    total = tb[ni:n_all, h, ch].astype(F32)
    for i in range(NY - 1):
        total = total + rb[i].astype(F32)
    sb[...] = total.astype(BF16).reshape(ni, NX, piece, LANES)
    for s in range(1, NX):
        i = s - 1
        to = (x + s) % NX
        c = remote(sb.at[:, to], qb.at[i], p2_send.at[1, i], p2_recv.at[1, i], at(to, y))
        c.start()
        second_sum.append(c)
    for c in second_sum[: NY - 1]:
        c.wait_recv()
    total = sa[:, h, ch].astype(F32)
    for i in range(NY - 1):
        total = total + qa[i].astype(F32)
    fb[0:ni] = total.astype(BF16)
    for c in second_sum[NY - 1 :]:
        c.wait_recv()
    total = sb[:, x].astype(F32)
    for i in range(NX - 1):
        total = total + qb[i].astype(F32)
    fb[ni:n_all] = total.astype(BF16)

    for n in range(n_all):
        goal = core * half + n * NH + h
        step = (z + nz - goal) % nz

        @pl.when(step != 0)
        def _():
            remote(fb.at[n], zb.at[step], z_send.at[n], z_recv.at[0], (me, goal)).start()

        @pl.when(step == 0)
        def _():
            zb[0] = fb[n]

    @pl.when(is_src)
    def _():
        rest = zb.at[1:nz]
        remote(rest, rest, z_send.at[0], z_recv.at[0], (me, (z + 1) % nz)).wait_recv()
        whole = zb[0].astype(F32)
        for i in range(1, nz):
            whole = whole + zb[i].astype(F32)
        gb[x, ch] = whole.astype(BF16)

        def send_piece(s, carry):
            dst = gb.at[x, ch]
            remote(
                dst, dst, g_send.at[s - 1], g_recv.at[x * 2 + ch], ((me + s) % ndp, z)
            ).start()
            return carry

        lax.fori_loop(1, ndp, send_piece, 0)

    arrived = pr.at[1:ndp]
    remote(ps.at[1:ndp], arrived, ps_sem.at[0], ps_sem.at[1], (sib, z)).wait()
    remote(ks.at[1:ndp], kr.at[1:ndp], kk_sem.at[0], kk_sem.at[1], (sib, z)).wait()
    begin = jnp.concatenate([pr[...], pr[...]], axis=1)
    place = begin + lax.broadcasted_iota(jnp.int32, begin.shape, 1).astype(F32)
    lane = lax.broadcasted_iota(jnp.int32, begin.shape, 2).astype(F32)
    put = jnp.where(place == lane, 1.0, 0.0).astype(BF16).reshape(n_slots, LANES)
    kg_ref[...] = lax.dot_general(
        put, kr[...].reshape(n_slots, 256), TN, preferred_element_type=F32
    ).astype(BF16)

    for xx in range(NX):
        for c in range(2):
            is_mine = jnp.logical_and(x == xx, ch == c)

            @pl.when(jnp.logical_not(jnp.logical_and(is_src, is_mine)))
            def _():
                dst = gb.at[xx, c]
                remote(dst, dst, g_send.at[0], g_recv.at[xx * 2 + c], (sib, z)).wait_recv()

            wg_ref[xx * piece : (xx + 1) * piece, c * LANES : (c + 1) * LANES] = gb[
                xx, c
            ].astype(F32)

    x_sib.wait_send()
    vp_copy.wait_send()
    for c, r in w_small + w_large:
        c.wait_send()
    for c in first_sum + second_sum:
        c.wait_send()
    for n in range(n_all):
        goal = core * half + n * NH + h

        @pl.when(goal != z)
        def _():
            remote(fb.at[n], zb.at[1], z_send.at[n], z_recv.at[0], (me, goal)).wait_send()

    @pl.when(is_src)
    def _():
        def sent_weight(s, carry):
            dst = wf.at[own_n, h, ch, xrows(x)]
            remote(
                w_piece, dst, wz_send.at[s - 1], wz_recv.at[own_n], (me, (z + s) % nz)
            ).wait_send()
            return carry

        lax.fori_loop(1, nz, sent_weight, 0)

        def sent_piece(s, carry):
            dst = gb.at[x, ch]
            remote(
                dst, dst, g_send.at[s - 1], g_recv.at[x * 2 + ch], ((me + s) % ndp, z)
            ).wait_send()
            return carry

        lax.fori_loop(1, ndp, sent_piece, 0)


def on_device(
    layer_input,
    queries,
    key_states,
    upstream,
    advantage,
    value_weight,
    row_sample,
    row_rank,
    row_pack,
):
    nz = lax.axis_size("fsdp")
    ndp = NX * NY * CORES
    own, depth = layer_input.shape
    shard, kv_width = value_weight.shape
    piece = shard // NX
    width = depth // 2
    n_all = nz // 2 // NH
    ni = n_all // 2
    vmem = pltpu.VMEM
    dma = pltpu.SemaphoreType.DMA
    hbm = pl.BlockSpec(memory_space=pl.ANY)
    inside = pl.BlockSpec(memory_space=pltpu.VMEM)
    kept = [nk for _, _, nk in BLOCKS]
    return pl.pallas_call(
        functools.partial(kernel, nz),
        out_shape=(
            jax.ShapeDtypeStruct((BAL, kv_width), BF16),
            jax.ShapeDtypeStruct((shard, kv_width), F32),
        ),
        in_specs=[hbm] * 5 + [inside] * 4,
        out_specs=(inside, inside),
        scratch_shapes=[
            vmem(queries.shape, BF16),
            vmem(upstream.shape, BF16),
            vmem((own, kv_width), BF16),
            vmem((2, own, width), BF16),
            vmem((n_all, NH, 2, shard, LANES), BF16),
            vmem((KV_HEADS, 4, own, 256), BF16),
            vmem((8, 4, kept[0], LANES), F32),
            vmem((8, 4, kept[1], LANES), F32),
            vmem((kept[0], LANES), F32),
            vmem((kept[1], LANES), F32),
            vmem((2, 1, LANES), F32),
            vmem((KV_HEADS, own, LANES), F32),
            vmem((own, kv_width), BF16),
            vmem((own, kv_width), BF16),
            vmem((n_all, NH * shard, kv_width), F32),
            vmem((n_all, NH, 2, shard, LANES), BF16),
            vmem((NX - 1, ni, NH, 2, piece, LANES), BF16),
            vmem((NY - 1, ni, shard, LANES), BF16),
            vmem((ni, NH, 2, piece, LANES), BF16),
            vmem((ni, NX, piece, LANES), BF16),
            vmem((NY - 1, ni, piece, LANES), BF16),
            vmem((NX - 1, ni, piece, LANES), BF16),
            vmem((n_all, piece, LANES), BF16),
            vmem((nz, piece, LANES), BF16),
            vmem((NX, 2, piece, LANES), BF16),
            vmem((2, own, kv_width), F32),
            vmem((own, kv_width), F32),
            vmem((ndp * MAXLEN, own), BF16),
            vmem((ndp, MAXLEN, kv_width), BF16),
            vmem((ndp, MAXLEN, kv_width), BF16),
            vmem((ndp, 8, LANES), F32),
            vmem((ndp, 8, LANES), F32),
            dma((5,)),
            dma((2,)),
            dma((2,)),
            dma((2,)),
            dma((nz - 1,)),
            dma((n_all,)),
            dma((2, max(NX, NY) - 1)),
            dma((2, max(NX, NY) - 1)),
            dma((2, max(NX, NY) - 1)),
            dma((2, max(NX, NY) - 1)),
            dma((2, max(NX, NY) - 1)),
            dma((2, max(NX, NY) - 1)),
            dma((2, max(NX, NY) - 1)),
            dma((2, max(NX, NY) - 1)),
            dma((n_all,)),
            dma((1,)),
            dma((ndp - 1,)),
            dma((2 * NX,)),
            dma((2,)),
            dma((2,)),
        ],
        compiler_params=pltpu.CompilerParams(
            collective_id=0, has_side_effects=True, vmem_limit_bytes=48 * 1024 * 1024
        ),
    )(
        layer_input,
        queries,
        key_states,
        upstream,
        value_weight,
        advantage.reshape(1, own),
        row_sample.reshape(1, own),
        row_rank.reshape(1, own),
        row_pack.reshape(1, own),
    )


def solution(mesh):
    return jax.shard_map(
        on_device,
        mesh=mesh,
        in_specs=(
            P(("dp", "fsdp"), None),
            P(("dp", "fsdp"), None),
            P(("dp", "fsdp"), None),
            P(("dp", "fsdp"), None),
            P(("dp", "fsdp")),
            P("fsdp", None),
            P(("dp", "fsdp")),
            P(("dp", "fsdp")),
            P(("dp", "fsdp")),
        ),
        out_specs=(P(("dp", "fsdp"), None), P("fsdp", None)),
        check_vma=False,
    )
```

```python
import functools

import jax
import jax.numpy as jnp
from jax import lax
from jax.experimental import pallas as pl
from jax.experimental.pallas import tpu as pltpu
from jax.sharding import PartitionSpec as P

NX, NY, CORES = 4, 4, 2
KV_HEADS = 4
HEAD_DIM = 64
BAL = 128
MAXLEN = 16
LANES = 128
NH = NY // 2
MESH = pl.DeviceIdType.MESH
BF16, F32 = jnp.bfloat16, jnp.float32
NEG = -1e30
BLOCKS = ((0, 0, 128), (128, 112, 144))
NT = (((1,), (1,)), ((), ()))
TN = (((0,), (0,)), ((), ()))


def spread_heads(source, kb, scale):
    rows = source.shape[0]
    lane = lax.broadcasted_iota(jnp.int32, (rows, LANES), 1)
    zero = jnp.zeros((rows, LANES), BF16)
    for pair in range(2):
        tile = source[:, pair * LANES : (pair + 1) * LANES].astype(F32) * scale
        swapped = pltpu.roll(tile, HEAD_DIM, 1)
        for odd in range(2):
            g = 2 * pair + odd
            low = jnp.where(lane < HEAD_DIM, tile if odd == 0 else swapped, 0.0).astype(BF16)
            high = jnp.where(lane >= HEAD_DIM, tile if odd == 1 else swapped, 0.0).astype(BF16)
            for r in range(4):
                kb[g, r, :, pl.ds((r // 2) * LANES, LANES)] = low if r % 2 == 0 else high
                kb[g, r, :, pl.ds((1 - r // 2) * LANES, LANES)] = zero


def head_sum(parts, tiles, rows):
    even = jnp.concatenate([parts[i] for i in (0, 2, 4, 6)], axis=1)
    odd = jnp.concatenate([parts[i] for i in (1, 3, 5, 7)], axis=1)
    both = jnp.dot(
        jnp.concatenate([even, odd], axis=0),
        jnp.concatenate(tiles, axis=0),
        preferred_element_type=F32,
    )
    return both[:rows] + pltpu.roll(both[rows:], HEAD_DIM, 1)


def put_rows(acc, g, block, w):
    if block == 0:
        acc[g, 0:128, :] = w
    else:
        acc[g, 112:128, :] = acc[g, 112:128, :] + w[:16]
        acc[g, 128:256, :] = w[16:]


def join_pair(acc, pair):
    rows = acc.shape[1]
    lane = lax.broadcasted_iota(jnp.int32, (rows, LANES), 1)
    return jnp.where(
        lane < HEAD_DIM, acc[2 * pair], pltpu.roll(acc[2 * pair + 1], HEAD_DIM, 1)
    ).astype(BF16)


def kernel(
    nz,
    x_hbm,
    q_hbm,
    k_hbm,
    u_hbm,
    w_hbm,
    adv_hbm,
    samp_hbm,
    rank_hbm,
    pack_hbm,
    kg_ref,
    wg_ref,
    qv,
    uv,
    kv,
    xv,
    xs,
    adv_ref,
    samp_ref,
    rank_ref,
    pack_ref,
    wf,
    kb,
    p0,
    p1,
    bias0,
    bias1,
    frow,
    acc,
    vg,
    tacc,
    te,
    tr,
    tb,
    ra,
    rb,
    sa,
    sb,
    qa,
    qb,
    fb,
    zb,
    gb,
    vp,
    vp_sib,
    s1h,
    ks,
    kr,
    ps,
    pr,
    loc,
    x_sem,
    xs_sem,
    t_sem,
    vp_sem,
    wz_send,
    wz_recv,
    ws_send,
    ws_recv,
    wl_send,
    wl_recv,
    p1_send,
    p1_recv,
    p2_send,
    p2_recv,
    z_send,
    z_recv,
    g_send,
    g_recv,
    ps_sem,
    kk_sem,
):
    ndp = NX * NY * CORES
    half = nz // 2
    n_all = half // NH
    ni = n_all // 2
    own = q_hbm.shape[0]
    width = x_hbm.shape[1] // 2
    shard = w_hbm.shape[0]
    piece = shard // NX
    chunk = NH * shard
    me = lax.axis_index("dp")
    z = lax.axis_index("fsdp")
    core = me % CORES
    x = me // CORES // NY
    y = me // CORES % NY
    h, ch = y // 2, y % 2
    is_src = jnp.logical_and(z // half == core, z % NH == h)
    own_n = z % half // NH
    sib = me + 1 - 2 * core

    def at(dx, dy):
        return ((dx * NY + dy) * CORES + core, z)

    def xrows(dx):
        return pl.ds(pl.multiple_of(dx * piece, 16), piece)

    def remote(src, dst, send, recv, device):
        return pltpu.make_async_remote_copy(
            src_ref=src,
            dst_ref=dst,
            send_sem=send,
            recv_sem=recv,
            device_id=device,
            device_id_type=MESH,
        )

    barrier = pltpu.get_barrier_semaphore()

    def greet_z(s, carry):
        pl.semaphore_signal(barrier, inc=1, device_id=(me, (z + s) % nz), device_id_type=MESH)
        return carry

    def greet_dp(s, carry):
        pl.semaphore_signal(barrier, inc=1, device_id=((me + s) % ndp, z), device_id_type=MESH)
        return carry

    lax.fori_loop(1, nz, greet_z, 0)
    lax.fori_loop(1, ndp, greet_dp, 0)

    small = [
        pltpu.make_async_copy(src, dst, loc.at[i])
        for i, (src, dst) in enumerate(
            (
                (samp_hbm, samp_ref),
                (adv_hbm, adv_ref),
                (rank_hbm, rank_ref),
                (pack_hbm, pack_ref),
                (k_hbm, kv),
            )
        )
    ]
    middle = []
    for b in range(2):
        rows = pl.ds(b * LANES, LANES)
        middle.append(pltpu.make_async_copy(q_hbm.at[rows], qv.at[rows], loc.at[5 + 2 * b]))
        middle.append(pltpu.make_async_copy(u_hbm.at[rows], uv.at[rows], loc.at[6 + 2 * b]))
    wide = []
    for i in range(8):
        rows = pl.ds(i * (own // 8), own // 8)
        wide.append(pltpu.make_async_copy(x_hbm.at[rows], xv.at[rows], x_sem.at[i]))
    w_piece = w_hbm.at[xrows(x), pl.ds(pl.multiple_of(ch * LANES, LANES), LANES)]
    wcopy = pltpu.make_async_copy(w_piece, wf.at[own_n, h, ch, xrows(x)], loc.at[9])
    for c in small + middle + wide:
        c.start()

    @pl.when(is_src)
    def _():
        wcopy.start()

    for c in small:
        c.wait()
    samp = samp_ref[...].astype(F32)
    col = jnp.transpose(jnp.broadcast_to(samp, (LANES, own)))
    s_at = lax.broadcasted_iota(jnp.int32, (own, LANES), 0)
    live = samp >= 0
    slots = []
    for b, (t0, k0, nk) in enumerate(BLOCKS):
        same = col == samp[:, t0 : t0 + LANES]
        t_at = lax.broadcasted_iota(jnp.int32, (own, LANES), 1) + t0
        count = jnp.sum(jnp.where(same, 1.0, 0.0), axis=0, keepdims=True)
        slots.append(
            jnp.sum(jnp.where(jnp.logical_and(same, s_at < t_at), 1.0, 0.0), axis=0, keepdims=True)
        )
        bias = jnp.where(jnp.logical_and(same, s_at <= t_at), 0.0, NEG)
        (bias0, bias1)[b][...] = bias[k0 : k0 + nk]
        frow[b] = jnp.where(
            live[:, t0 : t0 + LANES], adv_ref[:, t0 : t0 + LANES] / count, 0.0
        )
    slot = jnp.concatenate(slots, axis=1)
    spread_heads(kv, kb, HEAD_DIM**-0.5)
    for c in middle:
        c.wait()

    def forward(g, carry):
        at_lane = g * 512
        for b, (t0, k0, nk) in enumerate(BLOCKS):
            keys = kb[g, :, k0 : k0 + nk, :].reshape(4 * nk, 256)
            bias = (bias0, bias1)[b][...]
            parts = []
            for part in range(2):
                lanes = pl.ds(pl.multiple_of(at_lane + part * 256, 256), 256)
                s = lax.dot_general(
                    keys, qv[t0 : t0 + LANES, lanes], NT, preferred_element_type=F32
                )
                s = s.reshape(4, nk, LANES) + bias[None]
                e = jnp.exp(s - jnp.max(s, axis=1, keepdims=True))
                soft = e * (1.0 / jnp.sum(e, axis=1, keepdims=True))
                (p0, p1)[b][g * 2 + part] = soft
                scaled = (soft * frow[b][None]).astype(BF16)
                parts += [scaled[r] for r in range(4)]
            tiles = [
                uv[t0 : t0 + LANES, pl.ds(pl.multiple_of(at_lane + i * LANES, LANES), LANES)]
                for i in range(4)
            ]
            put_rows(acc, g, b, head_sum(parts, tiles, nk))
        return carry

    lax.fori_loop(0, KV_HEADS, forward, 0)
    for pair in range(2):
        vg[:, pair * LANES : (pair + 1) * LANES] = join_pair(acc, pair)

    for c in wide:
        c.wait()

    def term(start, n):
        lanes = pl.ds(pl.multiple_of(start + n * chunk, LANES), chunk)
        t = lax.dot_general(xv[:, lanes], vg[...], TN, preferred_element_type=F32)
        return [t[:, c * LANES : (c + 1) * LANES].reshape(NH, shard, LANES) for c in range(2)]

    def term_other(n, carry):
        t = term((1 - core) * width, n)
        for c in range(2):
            te[n, :, c] = t[c].astype(BF16)
        return carry

    def term_own(n, carry):
        t = term(core * width, n)
        for c in range(2):
            tacc[n, :, c] = t[c]
        return carry

    lax.fori_loop(0, n_all, term_other, 0)

    pl.semaphore_wait(barrier, ndp - 1 + nz - 1)

    @pl.when(is_src)
    def _():
        def send(s, carry):
            remote(
                w_piece,
                wf.at[own_n, h, ch, xrows(x)],
                wz_send.at[s - 1],
                wz_recv.at[own_n],
                (me, (z + s) % nz),
            ).start()
            return carry

        lax.fori_loop(1, nz, send, 0)

    order = [n for i in range(ni) for n in (i, ni + i)]
    t_copies = [
        remote(te.at[n], tr.at[n], t_sem.at[0, n], t_sem.at[1, n], (sib, z)) for n in range(n_all)
    ]
    for n in order:
        t_copies[n].start()
    lax.fori_loop(0, n_all, term_own, 0)

    first_sum = {}
    for n in order:
        t_copies[n].wait_recv()
        tb[n] = (tacc[n] + tr[n].astype(F32)).astype(BF16)
        first_sum[n] = []
        for s in range(1, NX if n < ni else NY):
            i = s - 1
            if n < ni:
                to = (x + s) % NX
                c = remote(
                    tb.at[n, :, :, xrows(to)],
                    ra.at[n, i],
                    p1_send.at[n, i],
                    p1_recv.at[n, i],
                    at(to, y),
                )
            else:
                to = (y + s) % NY
                c = remote(
                    tb.at[n, to // 2, to % 2],
                    rb.at[n - ni, i],
                    p1_send.at[n, i],
                    p1_recv.at[n, i],
                    at(x, to),
                )
            c.start()
            first_sum[n].append(c)

    other = pl.ds(pl.multiple_of((1 - core) * width, LANES), width)
    x_sib = remote(xv.at[:, other], xs, xs_sem.at[0], xs_sem.at[1], (sib, z))
    x_sib.start()
    rank = rank_ref[...]
    rel = jnp.where(rank >= me, rank - me, rank - me + ndp)
    target = jnp.where(live, rel.astype(F32) * MAXLEN + slot, -1.0).astype(jnp.int32)
    n_slots = ndp * MAXLEN
    s1h[...] = jnp.where(
        lax.broadcasted_iota(jnp.int32, (n_slots, own), 0) == target, 1.0, 0.0
    ).astype(BF16)
    first = jnp.where(jnp.logical_and(live, slot == 0), rel, -1)
    pack = pack_ref[...].astype(F32)
    hit = lax.broadcasted_iota(jnp.int32, (ndp, 8, own), 0) == first[None]
    begin = jnp.sum(jnp.where(hit, pack[None], 0.0), axis=2, keepdims=True)
    ps[...] = jnp.broadcast_to(begin, (ndp, 8, LANES))
    pr[0] = ps[0]

    def send_begin(s, carry):
        remote(ps.at[s], pr.at[s], ps_sem.at[0], ps_sem.at[1], ((me + s) % ndp, z)).start()
        return carry

    lax.fori_loop(1, ndp, send_begin, 0)

    second_sum = {}

    def to_second(n):
        for c in first_sum[n]:
            c.wait_recv()
        second_sum[n] = []
        if n < ni:
            total = tb[n, :, :, xrows(x)].astype(F32)
            for i in range(NX - 1):
                total = total + ra[n, i].astype(F32)
            sa[n] = total.astype(BF16)
        else:
            total = tb[n, h, ch].astype(F32)
            for i in range(NY - 1):
                total = total + rb[n - ni, i].astype(F32)
            sb[n - ni] = total.astype(BF16).reshape(NX, piece, LANES)
        for s in range(1, NY if n < ni else NX):
            i = s - 1
            if n < ni:
                to = (y + s) % NY
                c = remote(
                    sa.at[n, to // 2, to % 2],
                    qa.at[n, i],
                    p2_send.at[n, i],
                    p2_recv.at[n, i],
                    at(x, to),
                )
            else:
                to = (x + s) % NX
                c = remote(
                    sb.at[n - ni, to],
                    qb.at[n - ni, i],
                    p2_send.at[n, i],
                    p2_recv.at[n, i],
                    at(to, y),
                )
            c.start()
            second_sum[n].append(c)

    def to_shard(n):
        for c in second_sum[n]:
            c.wait_recv()
        if n < ni:
            total = sa[n, h, ch].astype(F32)
            for i in range(NY - 1):
                total = total + qa[n, i].astype(F32)
        else:
            total = sb[n - ni, x].astype(F32)
            for i in range(NX - 1):
                total = total + qb[n - ni, i].astype(F32)
        fb[n] = total.astype(BF16)
        goal = core * half + n * NH + h
        step = (z + nz - goal) % nz

        @pl.when(step != 0)
        def _():
            remote(fb.at[n], zb.at[step], z_send.at[n], z_recv.at[0], (me, goal)).start()

        @pl.when(step == 0)
        def _():
            zb[0] = fb[n]

    for n in order[:2]:
        to_second(n)

    for n in range(n_all):
        @pl.when(jnp.logical_not(jnp.logical_and(is_src, own_n == n)))
        def _():
            dst = wf.at[n, h, ch, xrows(x)]
            remote(dst, dst, wz_send.at[0], wz_recv.at[n], (me, (z + 1) % nz)).wait_recv()

    @pl.when(is_src)
    def _():
        wcopy.wait()

    mine_a = wf.at[0:ni, h, ch, xrows(x)]
    mine_b = wf.at[ni:n_all, h, ch, xrows(x)]
    w_small = []
    for s in range(1, NY):
        i = s - 1
        to, src = (y + s) % NY, (y + NY - s) % NY
        c = remote(mine_a, mine_a, ws_send.at[0, i], ws_recv.at[0, i], at(x, to))
        c.start()
        dst = wf.at[0:ni, src // 2, src % 2, xrows(x)]
        w_small.append((c, remote(dst, dst, ws_send.at[0, i], ws_recv.at[0, i], at(x, src))))
    for s in range(1, NX):
        i = s - 1
        to, src = (x + s) % NX, (x + NX - s) % NX
        c = remote(mine_b, mine_b, ws_send.at[1, i], ws_recv.at[1, i], at(to, y))
        c.start()
        dst = wf.at[ni:n_all, h, ch, xrows(src)]
        w_small.append((c, remote(dst, dst, ws_send.at[1, i], ws_recv.at[1, i], at(src, y))))

    for n in order[2:]:
        to_second(n)
    for n in order[:2]:
        to_shard(n)

    for c, r in w_small:
        r.wait_recv()
    w_large = []
    line_a = wf.at[0:ni, :, :, xrows(x)]
    line_b = wf.at[ni:n_all, h, ch]
    for s in range(1, NX):
        i = s - 1
        to, src = (x + s) % NX, (x + NX - s) % NX
        c = remote(line_a, line_a, wl_send.at[0, i], wl_recv.at[0, i], at(to, y))
        c.start()
        dst = wf.at[0:ni, :, :, xrows(src)]
        w_large.append((c, remote(dst, dst, wl_send.at[0, i], wl_recv.at[0, i], at(src, y))))
    for s in range(1, NY):
        i = s - 1
        to, src = (y + s) % NY, (y + NY - s) % NY
        c = remote(line_b, line_b, wl_send.at[1, i], wl_recv.at[1, i], at(x, to))
        c.start()
        dst = wf.at[ni:n_all, src // 2, src % 2]
        w_large.append((c, remote(dst, dst, wl_send.at[1, i], wl_recv.at[1, i], at(x, src))))

    for n in order[2:]:
        to_shard(n)

    x_sib.wait_recv()
    for c, r in w_large:
        r.wait_recv()

    def weights():
        return jnp.concatenate([wf[:, :, c].reshape(width, LANES) for c in range(2)], axis=1)

    vp[1] = jnp.dot(xs[...], weights(), preferred_element_type=F32)
    vp_copy = remote(vp.at[1], vp_sib, vp_sem.at[0], vp_sem.at[1], (sib, z))
    vp_copy.start()
    mine = pl.ds(pl.multiple_of(core * width, LANES), width)
    vp[0] = jnp.dot(xv[:, mine], weights(), preferred_element_type=F32)

    @pl.when(is_src)
    def _():
        rest = zb.at[1:nz]
        remote(rest, rest, z_send.at[0], z_recv.at[0], (me, (z + 1) % nz)).wait_recv()
        whole = zb[0].astype(F32)
        for i in range(1, nz):
            whole = whole + zb[i].astype(F32)
        gb[x, ch] = whole.astype(BF16)

        def send_piece(s, carry):
            dst = gb.at[x, ch]
            remote(
                dst, dst, g_send.at[s - 1], g_recv.at[x * 2 + ch], ((me + s) % ndp, z)
            ).start()
            return carry

        lax.fori_loop(1, ndp, send_piece, 0)

    vp_copy.wait_recv()
    kv[...] = (vp[0] + vp_sib[...]).astype(BF16)
    spread_heads(kv, kb, 1.0)

    def backward(g, carry):
        at_lane = g * 512
        for b, (t0, k0, nk) in enumerate(BLOCKS):
            vals = kb[g, :, k0 : k0 + nk, :].reshape(4 * nk, 256)
            parts = []
            for part in range(2):
                lanes = pl.ds(pl.multiple_of(at_lane + part * 256, 256), 256)
                d = lax.dot_general(
                    vals, uv[t0 : t0 + LANES, lanes], NT, preferred_element_type=F32
                )
                d = d.reshape(4, nk, LANES)
                soft = (p0, p1)[b][g * 2 + part]
                delta = jnp.sum(soft * d, axis=1, keepdims=True)
                grad = soft * (d - delta) * (frow[b] * HEAD_DIM**-0.5)[None]
                grad = grad.astype(BF16)
                parts += [grad[r] for r in range(4)]
            tiles = [
                qv[t0 : t0 + LANES, pl.ds(pl.multiple_of(at_lane + i * LANES, LANES), LANES)]
                for i in range(4)
            ]
            put_rows(acc, g, b, head_sum(parts, tiles, nk))
        return carry

    for pair in range(2):
        lax.fori_loop(2 * pair, 2 * pair + 2, backward, 0)
        rows = jnp.dot(s1h[...], join_pair(acc, pair), preferred_element_type=F32)
        ks[pair] = rows.astype(BF16).reshape(ndp, MAXLEN, LANES)
        kr[pair, 0] = ks[pair, 0]

        def send_rows(s, carry):
            remote(
                ks.at[pair, s],
                kr.at[pair, s],
                kk_sem.at[pair, 0],
                kk_sem.at[pair, 1],
                ((me + s) % ndp, z),
            ).start()
            return carry

        lax.fori_loop(1, ndp, send_rows, 0)

    for xx in range(NX):
        for c in range(2):
            is_mine = jnp.logical_and(x == xx, ch == c)

            @pl.when(jnp.logical_not(jnp.logical_and(is_src, is_mine)))
            def _():
                dst = gb.at[xx, c]
                remote(dst, dst, g_send.at[0], g_recv.at[xx * 2 + c], (sib, z)).wait_recv()

            wg_ref[xx * piece : (xx + 1) * piece, c * LANES : (c + 1) * LANES] = gb[
                xx, c
            ].astype(F32)

    remote(ps.at[1:ndp], pr.at[1:ndp], ps_sem.at[0], ps_sem.at[1], (sib, z)).wait()
    begin = jnp.concatenate([pr[...], pr[...]], axis=1)
    place = begin + lax.broadcasted_iota(jnp.int32, begin.shape, 1).astype(F32)
    lane = lax.broadcasted_iota(jnp.int32, begin.shape, 2).astype(F32)
    put = jnp.where(place == lane, 1.0, 0.0).astype(BF16).reshape(n_slots, LANES)
    for pair in range(2):
        remote(
            ks.at[pair, 1:ndp],
            kr.at[pair, 1:ndp],
            kk_sem.at[pair, 0],
            kk_sem.at[pair, 1],
            (sib, z),
        ).wait()
        kg_ref[:, pair * LANES : (pair + 1) * LANES] = lax.dot_general(
            put, kr[pair].reshape(n_slots, LANES), TN, preferred_element_type=F32
        ).astype(BF16)

    x_sib.wait_send()
    vp_copy.wait_send()
    for c, r in w_small + w_large:
        c.wait_send()
    for n in range(n_all):
        t_copies[n].wait_send()
        for c in first_sum[n] + second_sum[n]:
            c.wait_send()
        goal = core * half + n * NH + h

        @pl.when(goal != z)
        def _():
            remote(fb.at[n], zb.at[1], z_send.at[n], z_recv.at[0], (me, goal)).wait_send()

    @pl.when(is_src)
    def _():
        def sent_weight(s, carry):
            dst = wf.at[own_n, h, ch, xrows(x)]
            remote(
                w_piece, dst, wz_send.at[s - 1], wz_recv.at[own_n], (me, (z + s) % nz)
            ).wait_send()
            return carry

        lax.fori_loop(1, nz, sent_weight, 0)

        def sent_piece(s, carry):
            dst = gb.at[x, ch]
            remote(
                dst, dst, g_send.at[s - 1], g_recv.at[x * 2 + ch], ((me + s) % ndp, z)
            ).wait_send()
            return carry

        lax.fori_loop(1, ndp, sent_piece, 0)


def on_device(
    layer_input,
    queries,
    key_states,
    upstream,
    advantage,
    value_weight,
    row_sample,
    row_rank,
    row_pack,
):
    nz = lax.axis_size("fsdp")
    ndp = NX * NY * CORES
    own, depth = layer_input.shape
    shard, kv_width = value_weight.shape
    piece = shard // NX
    width = depth // 2
    n_all = nz // 2 // NH
    ni = n_all // 2
    vmem = pltpu.VMEM
    dma = pltpu.SemaphoreType.DMA
    hbm = pl.BlockSpec(memory_space=pl.ANY)
    inside = pl.BlockSpec(memory_space=pltpu.VMEM)
    far = max(NX, NY) - 1
    kept = [nk for _, _, nk in BLOCKS]
    return pl.pallas_call(
        functools.partial(kernel, nz),
        out_shape=(
            jax.ShapeDtypeStruct((BAL, kv_width), BF16),
            jax.ShapeDtypeStruct((shard, kv_width), F32),
        ),
        in_specs=[hbm] * 9,
        out_specs=(inside, inside),
        scratch_shapes=[
            vmem(queries.shape, BF16),
            vmem(upstream.shape, BF16),
            vmem((own, kv_width), BF16),
            vmem((own, depth), BF16),
            vmem((own, width), BF16),
            vmem((1, own), F32),
            vmem((1, own), jnp.int32),
            vmem((1, own), jnp.int32),
            vmem((1, own), jnp.int32),
            vmem((n_all, NH, 2, shard, LANES), BF16),
            vmem((KV_HEADS, 4, own, 256), BF16),
            vmem((8, 4, kept[0], LANES), F32),
            vmem((8, 4, kept[1], LANES), F32),
            vmem((kept[0], LANES), F32),
            vmem((kept[1], LANES), F32),
            vmem((2, 1, LANES), F32),
            vmem((KV_HEADS, own, LANES), F32),
            vmem((own, kv_width), BF16),
            vmem((n_all, NH, 2, shard, LANES), F32),
            vmem((n_all, NH, 2, shard, LANES), BF16),
            vmem((n_all, NH, 2, shard, LANES), BF16),
            vmem((n_all, NH, 2, shard, LANES), BF16),
            vmem((ni, NX - 1, NH, 2, piece, LANES), BF16),
            vmem((ni, NY - 1, shard, LANES), BF16),
            vmem((ni, NH, 2, piece, LANES), BF16),
            vmem((ni, NX, piece, LANES), BF16),
            vmem((ni, NY - 1, piece, LANES), BF16),
            vmem((ni, NX - 1, piece, LANES), BF16),
            vmem((n_all, piece, LANES), BF16),
            vmem((nz, piece, LANES), BF16),
            vmem((NX, 2, piece, LANES), BF16),
            vmem((2, own, kv_width), F32),
            vmem((own, kv_width), F32),
            vmem((ndp * MAXLEN, own), BF16),
            vmem((2, ndp, MAXLEN, LANES), BF16),
            vmem((2, ndp, MAXLEN, LANES), BF16),
            vmem((ndp, 8, LANES), F32),
            vmem((ndp, 8, LANES), F32),
            dma((10,)),
            dma((8,)),
            dma((2,)),
            dma((2, n_all)),
            dma((2,)),
            dma((nz - 1,)),
            dma((n_all,)),
            dma((2, far)),
            dma((2, far)),
            dma((2, far)),
            dma((2, far)),
            dma((n_all, far)),
            dma((n_all, far)),
            dma((n_all, far)),
            dma((n_all, far)),
            dma((n_all,)),
            dma((1,)),
            dma((ndp - 1,)),
            dma((2 * NX,)),
            dma((2,)),
            dma((2, 2)),
        ],
        compiler_params=pltpu.CompilerParams(
            collective_id=0, has_side_effects=True, vmem_limit_bytes=62 * 1024 * 1024
        ),
    )(
        layer_input,
        queries,
        key_states,
        upstream,
        value_weight,
        advantage.reshape(1, own),
        row_sample.reshape(1, own),
        row_rank.reshape(1, own),
        row_pack.reshape(1, own),
    )


def solution(mesh):
    return jax.shard_map(
        on_device,
        mesh=mesh,
        in_specs=(
            P(("dp", "fsdp"), None),
            P(("dp", "fsdp"), None),
            P(("dp", "fsdp"), None),
            P(("dp", "fsdp"), None),
            P(("dp", "fsdp")),
            P("fsdp", None),
            P(("dp", "fsdp")),
            P(("dp", "fsdp")),
            P(("dp", "fsdp")),
        ),
        out_specs=(P(("dp", "fsdp"), None), P("fsdp", None)),
        check_vma=False,
    )
```

```python
import functools

import jax
import jax.numpy as jnp
from jax import lax
from jax.experimental import pallas as pl
from jax.experimental.pallas import tpu as pltpu
from jax.sharding import PartitionSpec as P

NX, NY, CORES = 4, 4, 2
KV_HEADS = 4
HEAD_DIM = 64
BAL = 128
MAXLEN = 16
LANES = 128
NH = NY // 2
MESH = pl.DeviceIdType.MESH
BF16, F32 = jnp.bfloat16, jnp.float32
NEG = -1e30
BLOCKS = ((0, 0, 128), (128, 112, 144))
NT = (((1,), (1,)), ((), ()))
TN = (((0,), (0,)), ((), ()))


def around(n):
    return sorted(range(1, n), key=lambda s: -min(s, n - s))


def spread_heads(source, kb, scale):
    rows = source.shape[0]
    lane = lax.broadcasted_iota(jnp.int32, (rows, LANES), 1)
    zero = jnp.zeros((rows, LANES), BF16)
    for pair in range(2):
        tile = source[:, pair * LANES : (pair + 1) * LANES].astype(F32) * scale
        swapped = pltpu.roll(tile, HEAD_DIM, 1)
        for odd in range(2):
            g = 2 * pair + odd
            low = jnp.where(lane < HEAD_DIM, tile if odd == 0 else swapped, 0.0).astype(BF16)
            high = jnp.where(lane >= HEAD_DIM, tile if odd == 1 else swapped, 0.0).astype(BF16)
            for r in range(4):
                kb[g, r, :, pl.ds((r // 2) * LANES, LANES)] = low if r % 2 == 0 else high
                kb[g, r, :, pl.ds((1 - r // 2) * LANES, LANES)] = zero


def head_sum(parts, tiles, rows):
    even = jnp.concatenate([parts[i] for i in (0, 2, 4, 6)], axis=1)
    odd = jnp.concatenate([parts[i] for i in (1, 3, 5, 7)], axis=1)
    both = jnp.dot(
        jnp.concatenate([even, odd], axis=0),
        jnp.concatenate(tiles, axis=0),
        preferred_element_type=F32,
    )
    return both[:rows] + pltpu.roll(both[rows:], HEAD_DIM, 1)


def put_rows(acc, g, block, w):
    if block == 0:
        acc[g, 0:128, :] = w
    else:
        acc[g, 112:128, :] = acc[g, 112:128, :] + w[:16]
        acc[g, 128:256, :] = w[16:]


def join_pair(acc, pair):
    rows = acc.shape[1]
    lane = lax.broadcasted_iota(jnp.int32, (rows, LANES), 1)
    return jnp.where(
        lane < HEAD_DIM, acc[2 * pair], pltpu.roll(acc[2 * pair + 1], HEAD_DIM, 1)
    ).astype(BF16)


def kernel(
    nz,
    x_hbm,
    q_hbm,
    k_hbm,
    u_hbm,
    w_hbm,
    adv_hbm,
    samp_hbm,
    rank_hbm,
    pack_hbm,
    kg_ref,
    wg_ref,
    qv,
    uv,
    kv,
    xv,
    xs,
    adv_ref,
    samp_ref,
    rank_ref,
    pack_ref,
    wf,
    kb,
    p0,
    p1,
    bias0,
    bias1,
    frow,
    acc,
    vg,
    tacc,
    te,
    tr,
    tb,
    ra,
    rb,
    ta,
    td,
    ca,
    cb,
    sa,
    sb,
    qa,
    qb,
    fb,
    zb,
    gb,
    gs,
    wgv,
    kgv,
    vp,
    vp_sib,
    s1h,
    ks,
    kr,
    ps,
    pr,
    put,
    ub,
    loc,
    x_sem,
    xs_sem,
    t_sem,
    vp_sem,
    wz_send,
    wz_recv,
    ws_send,
    ws_recv,
    wl_send,
    wl_recv,
    p1_send,
    p1_recv,
    p2_send,
    p2_recv,
    z_send,
    z_recv,
    g_send,
    g_recv,
    gf_sem,
    ps_sem,
    kk_sem,
):
    ndp = NX * NY * CORES
    half = nz // 2
    n_all = half // NH
    ni = n_all // 2
    own = q_hbm.shape[0]
    width = x_hbm.shape[1] // 2
    shard = w_hbm.shape[0]
    piece = shard // NX
    chunk = NH * shard
    me = lax.axis_index("dp")
    z = lax.axis_index("fsdp")
    core = me % CORES
    x = me // CORES // NY
    y = me // CORES % NY
    h, ch = y // 2, y % 2
    is_src = jnp.logical_and(z // half == core, z % NH == h)
    own_n = z % half // NH
    sib = me + 1 - 2 * core

    def at(dx, dy):
        return ((dx * NY + dy) * CORES + core, z)

    def xrows(dx):
        return pl.ds(pl.multiple_of(dx * piece, 16), piece)

    def remote(src, dst, send, recv, device):
        return pltpu.make_async_remote_copy(
            src_ref=src,
            dst_ref=dst,
            send_sem=send,
            recv_sem=recv,
            device_id=device,
            device_id_type=MESH,
        )

    def to_peers(send, carry=0):
        def step(i, carry):
            dx = (NX // 2 + (NX - 1) * (i // (NY * CORES))) % NX
            dy = (NY // 2 + (NY - 1) * (i // CORES % NY)) % NY
            dk = i % CORES
            place = ((x + dx) % NX * NY + (y + dy) % NY) * CORES + (core + dk) % CORES
            send((dx * NY + dy) * CORES + dk, (place, z))
            return carry

        here = (NX // 2 * NY + NY // 2) * CORES
        lax.fori_loop(0, here, step, 0)
        lax.fori_loop(here + 1, ndp, step, 0)

    def near_first(of_core):
        def distance(n):
            step = (z + nz - (of_core * half + n * NH)) % nz
            return jnp.minimum(step, nz - step)

        if ni == 1:
            return (0,), (1,)
        flip_a = (distance(1) < distance(0)).astype(jnp.int32)
        flip_b = (distance(3) < distance(2)).astype(jnp.int32)
        return (flip_a, 1 - flip_a), (2 + flip_b, 3 - flip_b)

    near_a, near_b = near_first(core)
    sib_a, sib_b = near_first(1 - core)
    far = [(near_a[i], near_b[i]) for i in reversed(range(ni))]
    near = [(near_a[i], near_b[i]) for i in range(ni)]

    barrier = pltpu.get_barrier_semaphore()

    def greet(s, device):
        pl.semaphore_signal(barrier, inc=1, device_id=device, device_id_type=MESH)

    for s in around(nz):
        greet(s, (me, (z + s) % nz))
    to_peers(greet)

    small = [
        pltpu.make_async_copy(src, dst, loc.at[i])
        for i, (src, dst) in enumerate(
            (
                (samp_hbm, samp_ref),
                (adv_hbm, adv_ref),
                (rank_hbm, rank_ref),
                (pack_hbm, pack_ref),
                (k_hbm, kv),
            )
        )
    ]
    middle = []
    for b in range(2):
        rows = pl.ds(b * LANES, LANES)
        middle.append(pltpu.make_async_copy(q_hbm.at[rows], qv.at[rows], loc.at[5 + 2 * b]))
        middle.append(pltpu.make_async_copy(u_hbm.at[rows], uv.at[rows], loc.at[6 + 2 * b]))
    wide = []
    for i in range(8):
        rows = pl.ds(i * (own // 8), own // 8)
        wide.append(pltpu.make_async_copy(x_hbm.at[rows], xv.at[rows], x_sem.at[i]))
    w_piece = w_hbm.at[xrows(x), pl.ds(pl.multiple_of(ch * LANES, LANES), LANES)]
    wcopy = pltpu.make_async_copy(w_piece, wf.at[own_n, h, ch, xrows(x)], loc.at[9])
    for c in small + middle + wide:
        c.start()

    @pl.when(is_src)
    def _():
        wcopy.start()

    for c in small:
        c.wait()
    samp = samp_ref[...].astype(F32)
    col = jnp.transpose(jnp.broadcast_to(samp, (LANES, own)))
    s_at = lax.broadcasted_iota(jnp.int32, (own, LANES), 0)
    live = samp >= 0
    slots = []
    for b, (t0, k0, nk) in enumerate(BLOCKS):
        same = col == samp[:, t0 : t0 + LANES]
        t_at = lax.broadcasted_iota(jnp.int32, (own, LANES), 1) + t0
        count = jnp.sum(jnp.where(same, 1.0, 0.0), axis=0, keepdims=True)
        slots.append(
            jnp.sum(jnp.where(jnp.logical_and(same, s_at < t_at), 1.0, 0.0), axis=0, keepdims=True)
        )
        bias = jnp.where(jnp.logical_and(same, s_at <= t_at), 0.0, NEG)
        (bias0, bias1)[b][...] = bias[k0 : k0 + nk]
        frow[b] = jnp.where(
            live[:, t0 : t0 + LANES], adv_ref[:, t0 : t0 + LANES] / count, 0.0
        )
    slot = jnp.concatenate(slots, axis=1)
    spread_heads(kv, kb, HEAD_DIM**-0.5)
    for c in middle:
        c.wait()

    def forward(g, carry):
        at_lane = g * 512
        for b, (t0, k0, nk) in enumerate(BLOCKS):
            keys = kb[g, :, k0 : k0 + nk, :].reshape(4 * nk, 256)
            bias = (bias0, bias1)[b][...]
            parts = []
            for part in range(2):
                lanes = pl.ds(pl.multiple_of(at_lane + part * 256, 256), 256)
                s = lax.dot_general(
                    keys, qv[t0 : t0 + LANES, lanes], NT, preferred_element_type=F32
                )
                s = s.reshape(4, nk, LANES) + bias[None]
                e = jnp.exp(s - jnp.max(s, axis=1, keepdims=True))
                soft = e * (1.0 / jnp.sum(e, axis=1, keepdims=True))
                (p0, p1)[b][g * 2 + part] = soft
                scaled = (soft * frow[b][None]).astype(BF16)
                parts += [scaled[r] for r in range(4)]
            tiles = [
                uv[t0 : t0 + LANES, pl.ds(pl.multiple_of(at_lane + i * LANES, LANES), LANES)]
                for i in range(4)
            ]
            put_rows(acc, g, b, head_sum(parts, tiles, nk))
        return carry

    lax.fori_loop(0, KV_HEADS, forward, 0, unroll=True)
    for pair in range(2):
        vg[:, pair * LANES : (pair + 1) * LANES] = join_pair(acc, pair)

    for c in wide:
        c.wait()

    def term(start, n):
        lanes = pl.ds(pl.multiple_of(start + n * chunk, LANES), chunk)
        t = lax.dot_general(xv[:, lanes], vg[...], TN, preferred_element_type=F32)
        return [t[:, c * LANES : (c + 1) * LANES].reshape(NH, shard, LANES) for c in range(2)]

    def term_other(n, carry):
        t = term((1 - core) * width, n)
        for c in range(2):
            te[n, :, c] = t[c].astype(BF16)
        return carry

    def term_own(n, carry):
        t = term(core * width, n)
        for c in range(2):
            tacc[n, :, c] = t[c]
        return carry

    lax.fori_loop(0, n_all, term_other, 0)

    pl.semaphore_wait(barrier, ndp - 1 + nz - 1)

    @pl.when(is_src)
    def _():
        for s in around(nz):
            remote(
                w_piece,
                wf.at[own_n, h, ch, xrows(x)],
                wz_send.at[s - 1],
                wz_recv.at[own_n],
                (me, (z + s) % nz),
            ).start()

    def exchange(n):
        return remote(te.at[n], tr.at[n], t_sem.at[0, n], t_sem.at[1, n], (sib, z))

    for i in reversed(range(ni)):
        exchange(sib_a[i]).start()
        exchange(sib_b[i]).start()
    lax.fori_loop(0, n_all, term_own, 0)

    def block(n, b, to, side):
        if b == 0:
            return tb.at[n, :, side, xrows(to)]
        return tb.at[n, to // 2, to % 2, pl.ds(side * (shard // 2), shard // 2)]

    def on_line(b, step):
        size = (NX, NY)[b]
        to = ((x, y)[b] + step + size) % size
        return to, (at(to, y) if b == 0 else at(x, to))

    def first_copy(n, b, i, src, dst, step):
        return remote(src, dst, p1_send.at[n, i], p1_recv.at[n, i], on_line(b, step)[1])

    def landing(n, b, slot, side):
        return ra.at[n, slot, :, side] if b == 0 else rb.at[n - ni, slot, side]

    def relay(n, b, side):
        return ta.at[n, side] if b == 0 else td.at[n - ni, side]

    def joined(n, b, side):
        return ca.at[n, side] if b == 0 else cb.at[n - ni, side]

    first_sum, first_relay = {}, {}
    for part in range(ni):
        for b in range(2):
            n = far[part][b]
            exchange(n).wait_recv()
            tb[n] = (tacc[n] + tr[n].astype(F32)).astype(BF16)
            right, left = on_line(b, 1)[0], on_line(b, -1)[0]
            two = on_line(b, 2)[0]
            if (NX, NY)[b] == 4:
                first_relay[part, b] = [
                    first_copy(n, b, 0, block(n, b, two, 0), relay(n, b, 0), 1),
                    first_copy(n, b, 1, block(n, b, two, 1), relay(n, b, 1), -1),
                ]
                first_sum[part, b] = [
                    first_copy(n, b, 2, block(n, b, right, 1), landing(n, b, 0, 1), 1),
                    first_copy(n, b, 3, block(n, b, left, 0), landing(n, b, 1, 0), -1),
                ]
            else:
                first_relay[part, b] = []
                first_sum[part, b] = [
                    first_copy(n, b, 2, block(n, b, right, 1), landing(n, b, 0, 1), 1),
                    first_copy(n, b, 4, block(n, b, right, 0), landing(n, b, 0, 0), 1),
                ]
            for c in first_relay[part, b] + first_sum[part, b]:
                c.start()

    for part in range(ni):
        for b in range(2):
            n = far[part][b]
            for side, c in enumerate(first_relay[part, b]):
                c.wait_recv()
                step = 1 - 2 * side
                goal = block(n, b, on_line(b, step)[0], side)
                here, both = relay(n, b, side), joined(n, b, side)
                both[...] = (goal[...].astype(F32) + here[...].astype(F32)).astype(BF16)
                c = first_copy(n, b, 4 + side, both, landing(n, b, side, side), step)
                c.start()
                first_sum[part, b].append(c)

    other = pl.ds(pl.multiple_of((1 - core) * width, LANES), width)
    x_sib = remote(xv.at[:, other], xs, xs_sem.at[0], xs_sem.at[1], (sib, z))
    x_sib.start()
    rank = rank_ref[...]
    dx = (lax.shift_right_logical(rank, (NY * CORES).bit_length() - 1) - x) & (NX - 1)
    dy = (lax.shift_right_logical(rank, CORES.bit_length() - 1) - y) & (NY - 1)
    rel = (dx * NY + dy) * CORES + ((rank - core) & (CORES - 1))
    target = jnp.where(live, rel.astype(F32) * MAXLEN + slot, -1.0).astype(jnp.int32)
    n_slots = ndp * MAXLEN
    s1h[...] = jnp.where(
        lax.broadcasted_iota(jnp.int32, (n_slots, own), 0) == target, 1.0, 0.0
    ).astype(BF16)
    first = jnp.where(jnp.logical_and(live, slot == 0), rel, -1)
    pack = pack_ref[...].astype(F32)
    hit = lax.broadcasted_iota(jnp.int32, (ndp, 8, own), 0) == first[None]
    begin = jnp.sum(jnp.where(hit, pack[None], 0.0), axis=2, keepdims=True)
    ps[...] = jnp.broadcast_to(begin, (ndp, 8, LANES))
    pr[0] = ps[0]

    def send_begin(s, device):
        remote(ps.at[s], pr.at[s], ps_sem.at[0], ps_sem.at[1], device).start()

    to_peers(send_begin)

    lane = lax.broadcasted_iota(jnp.int32, (own, LANES), 1)
    for head in range(8 * KV_HEADS):
        side = head // 8 % 2
        tile = uv[:, head // 2 * LANES : (head // 2 + 1) * LANES].astype(F32)
        if head % 2 != side:
            tile = pltpu.roll(tile, HEAD_DIM, 1)
        ub[head] = jnp.where(lane // HEAD_DIM == side, tile, 0.0).astype(BF16)

    second_sum = {}

    def to_second(part, b):
        n = far[part][b]
        for c in first_sum[part, b]:
            c.wait_recv()
        second_sum[part, b] = []
        slots = 2 if (NX, NY)[b] == 4 else 1
        if b == 0:
            total = tb[n, :, :, xrows(x)].astype(F32)
            for i in range(slots):
                total = total + ra[n, i].astype(F32)
            sa[n] = total.astype(BF16)
        else:
            total = tb[n, h, ch].astype(F32)
            for i in range(slots):
                total = total + rb[n - ni, i].astype(F32).reshape(shard, LANES)
            sb[n - ni] = total.astype(BF16).reshape(NX, piece, LANES)
        for s in around((NY, NX)[b]):
            i = s - 1
            if b == 0:
                to = (y + s) % NY
                c = remote(
                    sa.at[n, to // 2, to % 2],
                    qa.at[n, i],
                    p2_send.at[n, i],
                    p2_recv.at[n, i],
                    at(x, to),
                )
            else:
                to = (x + s) % NX
                c = remote(
                    sb.at[n - ni, to],
                    qb.at[n - ni, i],
                    p2_send.at[n, i],
                    p2_recv.at[n, i],
                    at(to, y),
                )
            c.start()
            second_sum[part, b].append(c)

    def to_shard(part, b):
        n = far[part][b]
        for c in second_sum[part, b]:
            c.wait_recv()
        if b == 0:
            total = sa[n, h, ch].astype(F32)
            for i in range(NY - 1):
                total = total + qa[n, i].astype(F32)
        else:
            total = sb[n - ni, x].astype(F32)
            for i in range(NX - 1):
                total = total + qb[n - ni, i].astype(F32)
        fb[n] = total.astype(BF16)
        goal = core * half + n * NH + h
        step = (z + nz - goal) % nz

        @pl.when(step != 0)
        def _():
            remote(fb.at[n], zb.at[step], z_send.at[n], z_recv.at[0], (me, goal)).start()

        @pl.when(step == 0)
        def _():
            zb[0] = fb[n]

    for b in range(2):
        to_second(0, b)

    @pl.when(is_src)
    def _():
        wcopy.wait()

    w_small, w_large = {}, {}
    for part in range(ni):
        for b in range(2):
            n = near[part][b]
            line = wf.at[n, h, ch, xrows(x)]

            @pl.when(jnp.logical_not(jnp.logical_and(is_src, own_n == n)))
            def _():
                remote(line, line, wz_send.at[0], wz_recv.at[n], (me, (z + 1) % nz)).wait_recv()

            w_small[part, b] = []
            for s in around((NY, NX)[b]):
                i = s - 1
                if b == 0:
                    to, src = at(x, (y + s) % NY), (y + NY - s) % NY
                    dst = wf.at[n, src // 2, src % 2, xrows(x)]
                else:
                    to, src = at((x + s) % NX, y), (x + NX - s) % NX
                    dst = wf.at[n, h, ch, xrows(src)]
                c = remote(line, line, ws_send.at[n, i], ws_recv.at[n, i], to)
                c.start()
                r = remote(dst, dst, ws_send.at[n, i], ws_recv.at[n, i], to)
                w_small[part, b].append((c, r))

    for part in range(1, ni):
        for b in range(2):
            to_second(part, b)
    for b in range(2):
        to_shard(0, b)

    def line_of(b, n, step, side=None):
        place = on_line(b, step)[0]
        if b == 0:
            return wf.at[n, :, :, xrows(place)] if side is None else wf.at[n, :, side, xrows(place)]
        if side is None:
            return wf.at[n, place // 2, place % 2]
        return wf.at[n, place // 2, place % 2, pl.ds(side * (shard // 2), shard // 2)]

    def w_copy(n, b, i, src, dst, step):
        send, recv, to = wl_send.at[n, i], wl_recv.at[n, i], on_line(b, step)[1]
        return remote(src, src, send, recv, to), remote(dst, dst, send, recv, to)

    for part in range(ni):
        for b in range(2):
            n = near[part][b]
            for c, r in w_small[part, b]:
                r.wait_recv()
            w_large[part, b] = [w_copy(n, b, 0, line_of(b, n, 0), line_of(b, n, -1), 1)]
            if (NX, NY)[b] == 4:
                w_large[part, b].append(w_copy(n, b, 1, line_of(b, n, 0), line_of(b, n, 1), -1))
            for c, r in w_large[part, b]:
                c.start()

    for part in range(1, ni):
        for b in range(2):
            to_shard(part, b)

    w_relay = {}
    for part in range(ni):
        for b in range(2):
            n = near[part][b]
            w_relay[part, b] = []
            for c, r in w_large[part, b]:
                r.wait_recv()
            if (NX, NY)[b] == 4:
                w_relay[part, b] = [
                    w_copy(n, b, 2, line_of(b, n, -1, 0), line_of(b, n, -2, 0), 1),
                    w_copy(n, b, 3, line_of(b, n, 1, 1), line_of(b, n, 2, 1), -1),
                ]
            for c, r in w_relay[part, b]:
                c.start()

    remote(ps.at[1:ndp], pr.at[1:ndp], ps_sem.at[0], ps_sem.at[1], (sib, z)).wait()
    begin = jnp.concatenate([pr[...], pr[...]], axis=1)
    place = begin + lax.broadcasted_iota(jnp.int32, begin.shape, 1).astype(F32)
    lane = lax.broadcasted_iota(jnp.int32, begin.shape, 2).astype(F32)
    put[...] = jnp.where(place == lane, 1.0, 0.0).astype(BF16).reshape(n_slots, LANES)

    x_sib.wait_recv()

    def values_of(n, rows):
        weights = jnp.concatenate([wf[n, :, c].reshape(chunk, LANES) for c in range(2)], axis=1)
        return jnp.dot(rows, weights, preferred_element_type=F32)

    def value_part(i, who):
        total = vp[who] if i > 0 else None
        for n in near[i]:
            if who == 1:
                rows = xs[:, pl.ds(pl.multiple_of(n * chunk, LANES), chunk)]
            else:
                rows = xv[:, pl.ds(pl.multiple_of(core * width + n * chunk, LANES), chunk)]
            part = values_of(n, rows)
            total = part if total is None else total + part
        vp[who] = total

    vp_copy = remote(vp.at[1], vp_sib, vp_sem.at[0], vp_sem.at[1], (sib, z))
    for i in range(ni):
        for b in range(2):
            for c, r in w_relay[i, b]:
                r.wait_recv()
        value_part(i, 1)
        if i == ni - 1:
            vp_copy.start()
        value_part(i, 0)

    def piece_copy(dx, dy, do):
        place = ((x + dx) % NX * NY + (y + dy) % NY) * CORES + ch

        @pl.when(place != me)
        def _():
            do(remote(gs, gb.at[ch, x], g_send.at[dx * NY + dy], g_recv.at[x], (place, z)))

    vp_copy.wait_recv()
    kv[...] = (vp[0] + vp_sib[...]).astype(BF16)

    @pl.when(is_src)
    def _():
        rest = zb.at[1:nz]
        remote(rest, rest, z_send.at[0], z_recv.at[0], (me, (z + 1) % nz)).wait_recv()
        whole = zb[0].astype(F32)
        for i in range(1, nz):
            whole = whole + zb[i].astype(F32)
        gs[...] = whole.astype(BF16)

        @pl.when(ch == core)
        def _():
            gb[ch, x] = whole.astype(BF16)

        for dx in around(NX) + [0]:
            for dy in around(NY) + [0]:
                piece_copy(dx, dy, lambda c: c.start())

    def backward(g):
        pair_lanes = slice(g // 2 * LANES, (g // 2 + 1) * LANES)
        for b, (t0, k0, nk) in enumerate(BLOCKS):
            vals = kv[k0 : k0 + nk, pair_lanes]
            scale = frow[b] * HEAD_DIM**-0.5
            parts = []
            for part in range(2):
                heads = ub[8 * g + 4 * part : 8 * g + 4 * part + 4, t0 : t0 + LANES, :]
                d = lax.dot_general(
                    vals, heads.reshape(4 * LANES, LANES), NT, preferred_element_type=F32
                )
                for r in range(4):
                    head = d[:, r * LANES : (r + 1) * LANES]
                    soft = (p0, p1)[b][g * 2 + part, r]
                    delta = jnp.sum(soft * head, axis=0, keepdims=True)
                    parts.append((soft * (head - delta) * scale).astype(BF16))
            tiles = [
                qv[t0 : t0 + LANES, g * 512 + i * LANES : g * 512 + (i + 1) * LANES]
                for i in range(4)
            ]
            put_rows(acc, g, b, head_sum(parts, tiles, nk))

    for pair in range(2):
        backward(2 * pair)
        backward(2 * pair + 1)
        rows = jnp.dot(s1h[...], join_pair(acc, pair), preferred_element_type=F32)
        ks[pair] = rows.astype(BF16).reshape(ndp, MAXLEN, LANES)
        kr[pair, 0] = ks[pair, 0]

        def send_rows(s, device):
            remote(
                ks.at[pair, s], kr.at[pair, s], kk_sem.at[pair, 0], kk_sem.at[pair, 1], device
            ).start()

        to_peers(send_rows)

    for xx in range(NX):
        is_mine = jnp.logical_and(x == xx, ch == core)

        @pl.when(jnp.logical_not(jnp.logical_and(is_src, is_mine)))
        def _():
            dst = gb.at[core, xx]
            remote(dst, dst, g_send.at[0], g_recv.at[xx], (sib, z)).wait_recv()

    g_copy = remote(gb.at[core], gb.at[core], gf_sem.at[0], gf_sem.at[1], (sib, z))
    g_copy.start()
    g_copy.wait_recv()
    for xx in range(NX):
        for c in range(2):
            wgv[xx * piece : (xx + 1) * piece, c * LANES : (c + 1) * LANES] = gb[c, xx].astype(F32)
    wg_copy = pltpu.make_async_copy(wgv, wg_ref, loc.at[0])
    wg_copy.start()

    for pair in range(2):
        remote(
            ks.at[pair, 1:ndp],
            kr.at[pair, 1:ndp],
            kk_sem.at[pair, 0],
            kk_sem.at[pair, 1],
            (sib, z),
        ).wait()
        kgv[:, pair * LANES : (pair + 1) * LANES] = lax.dot_general(
            put[...], kr[pair].reshape(n_slots, LANES), TN, preferred_element_type=F32
        ).astype(BF16)

    kg_copy = pltpu.make_async_copy(kgv, kg_ref, loc.at[1])
    kg_copy.start()

    x_sib.wait_send()
    vp_copy.wait_send()
    g_copy.wait_send()
    for n in range(n_all):
        exchange(n).wait_send()
        goal = core * half + n * NH + h

        @pl.when(goal != z)
        def _():
            remote(fb.at[n], zb.at[1], z_send.at[n], z_recv.at[0], (me, goal)).wait_send()

    for part in range(ni):
        for b in range(2):
            for c, r in w_small[part, b] + w_large[part, b] + w_relay[part, b]:
                c.wait_send()
            for c in first_relay[part, b] + first_sum[part, b] + second_sum[part, b]:
                c.wait_send()

    @pl.when(is_src)
    def _():
        def sent_weight(s, carry):
            dst = wf.at[own_n, h, ch, xrows(x)]
            remote(
                w_piece, dst, wz_send.at[s - 1], wz_recv.at[own_n], (me, (z + s) % nz)
            ).wait_send()
            return carry

        lax.fori_loop(1, nz, sent_weight, 0)

        for dx in range(NX):
            for dy in range(NY):
                piece_copy(dx, dy, lambda c: c.wait_send())

    wg_copy.wait()
    kg_copy.wait()


def on_device(
    layer_input,
    queries,
    key_states,
    upstream,
    advantage,
    value_weight,
    row_sample,
    row_rank,
    row_pack,
):
    nz = lax.axis_size("fsdp")
    ndp = NX * NY * CORES
    own, depth = layer_input.shape
    shard, kv_width = value_weight.shape
    piece = shard // NX
    width = depth // 2
    n_all = nz // 2 // NH
    ni = n_all // 2
    vmem = pltpu.VMEM
    dma = pltpu.SemaphoreType.DMA
    hbm = pl.BlockSpec(memory_space=pl.ANY)
    far = max(NX, NY) - 1
    kept = [nk for _, _, nk in BLOCKS]
    return pl.pallas_call(
        functools.partial(kernel, nz),
        out_shape=(
            jax.ShapeDtypeStruct((BAL, kv_width), BF16),
            jax.ShapeDtypeStruct((shard, kv_width), F32),
        ),
        in_specs=[hbm] * 9,
        out_specs=(hbm, hbm),
        scratch_shapes=[
            vmem(queries.shape, BF16),
            vmem(upstream.shape, BF16),
            vmem((own, kv_width), BF16),
            vmem((own, depth), BF16),
            vmem((own, width), BF16),
            vmem((1, own), F32),
            vmem((1, own), jnp.int32),
            vmem((1, own), jnp.int32),
            vmem((1, own), jnp.int32),
            vmem((n_all, NH, 2, shard, LANES), BF16),
            vmem((KV_HEADS, 4, own, 256), BF16),
            vmem((8, 4, kept[0], LANES), F32),
            vmem((8, 4, kept[1], LANES), F32),
            vmem((kept[0], LANES), F32),
            vmem((kept[1], LANES), F32),
            vmem((2, 1, LANES), F32),
            vmem((KV_HEADS, own, LANES), F32),
            vmem((own, kv_width), BF16),
            vmem((n_all, NH, 2, shard, LANES), F32),
            vmem((n_all, NH, 2, shard, LANES), BF16),
            vmem((n_all, NH, 2, shard, LANES), BF16),
            vmem((n_all, NH, 2, shard, LANES), BF16),
            vmem((ni, 2, NH, 2, piece, LANES), BF16),
            vmem((ni, 2, 2, shard // 2, LANES), BF16),
            vmem((ni, 2, NH, piece, LANES), BF16),
            vmem((ni, 2, shard // 2, LANES), BF16),
            vmem((ni, 2, NH, piece, LANES), BF16),
            vmem((ni, 2, shard // 2, LANES), BF16),
            vmem((ni, NH, 2, piece, LANES), BF16),
            vmem((ni, NX, piece, LANES), BF16),
            vmem((ni, NY - 1, piece, LANES), BF16),
            vmem((ni, NX - 1, piece, LANES), BF16),
            vmem((n_all, piece, LANES), BF16),
            vmem((nz, piece, LANES), BF16),
            vmem((2, NX, piece, LANES), BF16),
            vmem((piece, LANES), BF16),
            vmem((shard, kv_width), F32),
            vmem((BAL, kv_width), BF16),
            vmem((2, own, kv_width), F32),
            vmem((own, kv_width), F32),
            vmem((ndp * MAXLEN, own), BF16),
            vmem((2, ndp, MAXLEN, LANES), BF16),
            vmem((2, ndp, MAXLEN, LANES), BF16),
            vmem((ndp, 8, LANES), F32),
            vmem((ndp, 8, LANES), F32),
            vmem((ndp * MAXLEN, LANES), BF16),
            vmem((8 * KV_HEADS, own, LANES), BF16),
            dma((10,)),
            dma((8,)),
            dma((2,)),
            dma((2, n_all)),
            dma((2,)),
            dma((nz - 1,)),
            dma((n_all,)),
            dma((n_all, far)),
            dma((n_all, far)),
            dma((n_all, 4)),
            dma((n_all, 4)),
            dma((n_all, 6)),
            dma((n_all, 6)),
            dma((n_all, far)),
            dma((n_all, far)),
            dma((n_all,)),
            dma((1,)),
            dma((NX * NY,)),
            dma((NX,)),
            dma((2,)),
            dma((2,)),
            dma((2, 2)),
        ],
        compiler_params=pltpu.CompilerParams(
            collective_id=0, has_side_effects=True, vmem_limit_bytes=62 * 1024 * 1024
        ),
    )(
        layer_input,
        queries,
        key_states,
        upstream,
        value_weight,
        advantage.reshape(1, own),
        row_sample.reshape(1, own),
        row_rank.reshape(1, own),
        row_pack.reshape(1, own),
    )


def solution(mesh):
    return jax.shard_map(
        on_device,
        mesh=mesh,
        in_specs=(
            P(("dp", "fsdp"), None),
            P(("dp", "fsdp"), None),
            P(("dp", "fsdp"), None),
            P(("dp", "fsdp"), None),
            P(("dp", "fsdp")),
            P("fsdp", None),
            P(("dp", "fsdp")),
            P(("dp", "fsdp")),
            P(("dp", "fsdp")),
        ),
        out_specs=(P(("dp", "fsdp"), None), P("fsdp", None)),
        check_vma=False,
    )
```

```python
import functools

import jax
import jax.numpy as jnp
from jax import lax
from jax.experimental import pallas as pl
from jax.experimental.pallas import tpu as pltpu
from jax.sharding import PartitionSpec as P

NX, NY, CORES = 4, 4, 2
KV_HEADS = 4
HEAD_DIM = 64
BAL = 128
MAXLEN = 16
LANES = 128
NH = NY // 2
MESH = pl.DeviceIdType.MESH
BF16, F32 = jnp.bfloat16, jnp.float32
NEG = -1e30
BLOCKS = ((0, 0, 128), (128, 112, 144))
NT = (((1,), (1,)), ((), ()))
TN = (((0,), (0,)), ((), ()))


def around(n):
    return sorted(range(1, n), key=lambda s: -min(s, n - s))


def spread_heads(source, kb, scale):
    rows = source.shape[0]
    lane = lax.broadcasted_iota(jnp.int32, (rows, LANES), 1)
    zero = jnp.zeros((rows, LANES), BF16)
    for pair in range(2):
        tile = source[:, pair * LANES : (pair + 1) * LANES].astype(F32) * scale
        swapped = pltpu.roll(tile, HEAD_DIM, 1)
        for odd in range(2):
            g = 2 * pair + odd
            low = jnp.where(lane < HEAD_DIM, tile if odd == 0 else swapped, 0.0).astype(BF16)
            high = jnp.where(lane >= HEAD_DIM, tile if odd == 1 else swapped, 0.0).astype(BF16)
            for r in range(4):
                kb[g, r, :, pl.ds((r // 2) * LANES, LANES)] = low if r % 2 == 0 else high
                kb[g, r, :, pl.ds((1 - r // 2) * LANES, LANES)] = zero


def head_sum(parts, tiles, rows):
    even = jnp.concatenate([parts[i] for i in (0, 2, 4, 6)], axis=1)
    odd = jnp.concatenate([parts[i] for i in (1, 3, 5, 7)], axis=1)
    both = jnp.dot(
        jnp.concatenate([even, odd], axis=0),
        jnp.concatenate(tiles, axis=0),
        preferred_element_type=F32,
    )
    return both[:rows] + pltpu.roll(both[rows:], HEAD_DIM, 1)


def put_rows(acc, g, block, w):
    if block == 0:
        acc[g, 0:128, :] = w
    else:
        acc[g, 112:128, :] = acc[g, 112:128, :] + w[:16]
        acc[g, 128:256, :] = w[16:]


def join_pair(acc, pair):
    rows = acc.shape[1]
    lane = lax.broadcasted_iota(jnp.int32, (rows, LANES), 1)
    return jnp.where(
        lane < HEAD_DIM, acc[2 * pair], pltpu.roll(acc[2 * pair + 1], HEAD_DIM, 1)
    ).astype(BF16)


def kernel(
    nz,
    x_hbm,
    q_hbm,
    k_hbm,
    u_hbm,
    w_hbm,
    adv_hbm,
    samp_hbm,
    rank_hbm,
    pack_hbm,
    kg_ref,
    wg_ref,
    qv,
    uv,
    kv,
    xv,
    xs,
    adv_ref,
    samp_ref,
    rank_ref,
    pack_ref,
    wf,
    kb,
    p0,
    p1,
    bias0,
    bias1,
    frow,
    acc,
    vg,
    tacc,
    te,
    tr,
    tb,
    ra,
    rb,
    ta,
    td,
    ca,
    cb,
    sa,
    sb,
    qa,
    qb,
    fb,
    zb,
    gb,
    gs,
    wgv,
    kgv,
    vp,
    vp_sib,
    s1h,
    ks,
    kr,
    ps,
    pr,
    put,
    ub,
    loc,
    x_sem,
    xs_sem,
    t_sem,
    vp_sem,
    wz_send,
    wz_recv,
    ws_send,
    ws_recv,
    wl_send,
    wl_recv,
    p1_send,
    p1_recv,
    p2_send,
    p2_recv,
    z_send,
    z_recv,
    g_send,
    g_recv,
    gf_sem,
    ps_sem,
    kk_sem,
):
    ndp = NX * NY * CORES
    half = nz // 2
    n_all = half // NH
    ni = n_all // 2
    own = q_hbm.shape[0]
    width = x_hbm.shape[1] // 2
    shard = w_hbm.shape[0]
    piece = shard // NX
    chunk = NH * shard
    me = lax.axis_index("dp")
    z = lax.axis_index("fsdp")
    core = me % CORES
    x = me // CORES // NY
    y = me // CORES % NY
    h, ch = y // 2, y % 2
    is_src = jnp.logical_and(z // half == core, z % NH == h)
    own_n = z % half // NH
    sib = me + 1 - 2 * core

    def at(dx, dy):
        return ((dx * NY + dy) * CORES + core, z)

    def xrows(dx):
        return pl.ds(pl.multiple_of(dx * piece, 16), piece)

    def remote(src, dst, send, recv, device):
        return pltpu.make_async_remote_copy(
            src_ref=src,
            dst_ref=dst,
            send_sem=send,
            recv_sem=recv,
            device_id=device,
            device_id_type=MESH,
        )

    def to_peers(send, carry=0):
        def step(i, carry):
            dx = (NX // 2 + (NX - 1) * (i // (NY * CORES))) % NX
            dy = (NY // 2 + (NY - 1) * (i // CORES % NY)) % NY
            dk = i % CORES
            place = ((x + dx) % NX * NY + (y + dy) % NY) * CORES + (core + dk) % CORES
            send((dx * NY + dy) * CORES + dk, (place, z))
            return carry

        here = (NX // 2 * NY + NY // 2) * CORES
        lax.fori_loop(0, here, step, 0)
        lax.fori_loop(here + 1, ndp, step, 0)

    def near_first(of_core):
        def distance(n):
            step = (z + nz - (of_core * half + n * NH)) % nz
            return jnp.minimum(step, nz - step)

        if ni == 1:
            return (0,), (1,)
        flip_a = (distance(1) < distance(0)).astype(jnp.int32)
        flip_b = (distance(3) < distance(2)).astype(jnp.int32)
        return (flip_a, 1 - flip_a), (2 + flip_b, 3 - flip_b)

    near_a, near_b = near_first(core)
    sib_a, sib_b = near_first(1 - core)
    far = [(near_a[i], near_b[i]) for i in reversed(range(ni))]
    near = [(near_a[i], near_b[i]) for i in range(ni)]

    barrier = pltpu.get_barrier_semaphore()

    def greet(s, device):
        pl.semaphore_signal(barrier, inc=1, device_id=device, device_id_type=MESH)

    for s in around(nz):
        greet(s, (me, (z + s) % nz))
    to_peers(greet)

    small = [
        pltpu.make_async_copy(src, dst, loc.at[i])
        for i, (src, dst) in enumerate(
            (
                (samp_hbm, samp_ref),
                (adv_hbm, adv_ref),
                (rank_hbm, rank_ref),
                (pack_hbm, pack_ref),
                (k_hbm, kv),
            )
        )
    ]
    middle = []
    for b in range(2):
        rows = pl.ds(b * LANES, LANES)
        middle.append(pltpu.make_async_copy(q_hbm.at[rows], qv.at[rows], loc.at[5 + 2 * b]))
        middle.append(pltpu.make_async_copy(u_hbm.at[rows], uv.at[rows], loc.at[6 + 2 * b]))
    wide = []
    for i in range(8):
        rows = pl.ds(i * (own // 8), own // 8)
        wide.append(pltpu.make_async_copy(x_hbm.at[rows], xv.at[rows], x_sem.at[i]))
    w_piece = w_hbm.at[xrows(x), pl.ds(pl.multiple_of(ch * LANES, LANES), LANES)]
    wcopy = pltpu.make_async_copy(w_piece, wf.at[own_n, h, ch, xrows(x)], loc.at[9])
    for c in small + middle + wide:
        c.start()

    @pl.when(is_src)
    def _():
        wcopy.start()

    for c in small:
        c.wait()
    samp = samp_ref[...].astype(F32)
    col = jnp.transpose(jnp.broadcast_to(samp, (LANES, own)))
    s_at = lax.broadcasted_iota(jnp.int32, (own, LANES), 0)
    live = samp >= 0
    slots = []
    for b, (t0, k0, nk) in enumerate(BLOCKS):
        same = col == samp[:, t0 : t0 + LANES]
        t_at = lax.broadcasted_iota(jnp.int32, (own, LANES), 1) + t0
        count = jnp.sum(jnp.where(same, 1.0, 0.0), axis=0, keepdims=True)
        slots.append(
            jnp.sum(jnp.where(jnp.logical_and(same, s_at < t_at), 1.0, 0.0), axis=0, keepdims=True)
        )
        bias = jnp.where(jnp.logical_and(same, s_at <= t_at), 0.0, NEG)
        (bias0, bias1)[b][...] = bias[k0 : k0 + nk]
        frow[b] = jnp.where(
            live[:, t0 : t0 + LANES], adv_ref[:, t0 : t0 + LANES] / count, 0.0
        )
    slot = jnp.concatenate(slots, axis=1)
    spread_heads(kv, kb, HEAD_DIM**-0.5)
    for c in middle:
        c.wait()

    def forward(g, carry):
        at_lane = g * 512
        for b, (t0, k0, nk) in enumerate(BLOCKS):
            keys = kb[g, :, k0 : k0 + nk, :].reshape(4 * nk, 256)
            bias = (bias0, bias1)[b][...]
            parts = []
            for part in range(2):
                lanes = pl.ds(pl.multiple_of(at_lane + part * 256, 256), 256)
                s = lax.dot_general(
                    keys, qv[t0 : t0 + LANES, lanes], NT, preferred_element_type=F32
                )
                s = s.reshape(4, nk, LANES) + bias[None]
                e = jnp.exp(s - jnp.max(s, axis=1, keepdims=True))
                soft = e * (1.0 / jnp.sum(e, axis=1, keepdims=True))
                (p0, p1)[b][g * 2 + part] = soft
                scaled = (soft * frow[b][None]).astype(BF16)
                parts += [scaled[r] for r in range(4)]
            tiles = [
                uv[t0 : t0 + LANES, pl.ds(pl.multiple_of(at_lane + i * LANES, LANES), LANES)]
                for i in range(4)
            ]
            put_rows(acc, g, b, head_sum(parts, tiles, nk))
        return carry

    lax.fori_loop(0, KV_HEADS, forward, 0, unroll=True)
    for pair in range(2):
        vg[:, pair * LANES : (pair + 1) * LANES] = join_pair(acc, pair)

    for c in wide:
        c.wait()

    def term(start, n):
        lanes = pl.ds(pl.multiple_of(start + n * chunk, LANES), chunk)
        t = lax.dot_general(xv[:, lanes], vg[...], TN, preferred_element_type=F32)
        return [t[:, c * LANES : (c + 1) * LANES].reshape(NH, shard, LANES) for c in range(2)]

    def term_other(n, carry):
        t = term((1 - core) * width, n)
        for c in range(2):
            te[n, :, c] = t[c].astype(BF16)
        return carry

    def term_own(n, carry):
        t = term(core * width, n)
        for c in range(2):
            tacc[n, :, c] = t[c]
        return carry

    lax.fori_loop(0, n_all, term_other, 0)

    pl.semaphore_wait(barrier, ndp - 1 + nz - 1)

    @pl.when(is_src)
    def _():
        for s in around(nz):
            remote(
                w_piece,
                wf.at[own_n, h, ch, xrows(x)],
                wz_send.at[s - 1],
                wz_recv.at[own_n],
                (me, (z + s) % nz),
            ).start()

    def exchange(n):
        return remote(te.at[n], tr.at[n], t_sem.at[0, n], t_sem.at[1, n], (sib, z))

    for i in reversed(range(ni)):
        exchange(sib_a[i]).start()
        exchange(sib_b[i]).start()
    lax.fori_loop(0, n_all, term_own, 0)

    def block(n, b, to, side):
        if b == 0:
            return tb.at[n, :, side, xrows(to)]
        return tb.at[n, to // 2, to % 2, pl.ds(side * (shard // 2), shard // 2)]

    def on_line(b, step):
        size = (NX, NY)[b]
        to = ((x, y)[b] + step + size) % size
        return to, (at(to, y) if b == 0 else at(x, to))

    def first_copy(n, b, i, src, dst, step):
        return remote(src, dst, p1_send.at[n, i], p1_recv.at[n, i], on_line(b, step)[1])

    def landing(n, b, slot, side):
        return ra.at[n, slot, :, side] if b == 0 else rb.at[n - ni, slot, side]

    def relay(n, b, side):
        return ta.at[n, side] if b == 0 else td.at[n - ni, side]

    def joined(n, b, side):
        return ca.at[n, side] if b == 0 else cb.at[n - ni, side]

    first_sum, first_relay = {}, {}
    for part in range(ni):
        for b in range(2):
            n = far[part][b]
            exchange(n).wait_recv()
            tb[n] = (tacc[n] + tr[n].astype(F32)).astype(BF16)
            right, left = on_line(b, 1)[0], on_line(b, -1)[0]
            two = on_line(b, 2)[0]
            if (NX, NY)[b] == 4:
                first_relay[part, b] = [
                    first_copy(n, b, 0, block(n, b, two, 0), relay(n, b, 0), 1),
                    first_copy(n, b, 1, block(n, b, two, 1), relay(n, b, 1), -1),
                ]
                first_sum[part, b] = [
                    first_copy(n, b, 2, block(n, b, right, 1), landing(n, b, 0, 1), 1),
                    first_copy(n, b, 3, block(n, b, left, 0), landing(n, b, 1, 0), -1),
                ]
            else:
                first_relay[part, b] = []
                first_sum[part, b] = [
                    first_copy(n, b, 2, block(n, b, right, 1), landing(n, b, 0, 1), 1),
                    first_copy(n, b, 4, block(n, b, right, 0), landing(n, b, 0, 0), 1),
                ]
            for c in first_relay[part, b] + first_sum[part, b]:
                c.start()

    for part in range(ni):
        for b in range(2):
            n = far[part][b]
            for side, c in enumerate(first_relay[part, b]):
                c.wait_recv()
                step = 1 - 2 * side
                goal = block(n, b, on_line(b, step)[0], side)
                here, both = relay(n, b, side), joined(n, b, side)
                both[...] = (goal[...].astype(F32) + here[...].astype(F32)).astype(BF16)
                c = first_copy(n, b, 4 + side, both, landing(n, b, side, side), step)
                c.start()
                first_sum[part, b].append(c)

    other = pl.ds(pl.multiple_of((1 - core) * width, LANES), width)
    x_sib = remote(xv.at[:, other], xs, xs_sem.at[0], xs_sem.at[1], (sib, z))
    x_sib.start()
    second_sum = {}

    def to_second(part, b):
        n = far[part][b]
        for c in first_sum[part, b]:
            c.wait_recv()
        second_sum[part, b] = []
        slots = 2 if (NX, NY)[b] == 4 else 1
        if b == 0:
            total = tb[n, :, :, xrows(x)].astype(F32)
            for i in range(slots):
                total = total + ra[n, i].astype(F32)
            sa[n] = total.astype(BF16)
        else:
            total = tb[n, h, ch].astype(F32)
            for i in range(slots):
                total = total + rb[n - ni, i].astype(F32).reshape(shard, LANES)
            sb[n - ni] = total.astype(BF16).reshape(NX, piece, LANES)
        for s in around((NY, NX)[b]):
            i = s - 1
            if b == 0:
                to = (y + s) % NY
                c = remote(
                    sa.at[n, to // 2, to % 2],
                    qa.at[n, i],
                    p2_send.at[n, i],
                    p2_recv.at[n, i],
                    at(x, to),
                )
            else:
                to = (x + s) % NX
                c = remote(
                    sb.at[n - ni, to],
                    qb.at[n - ni, i],
                    p2_send.at[n, i],
                    p2_recv.at[n, i],
                    at(to, y),
                )
            c.start()
            second_sum[part, b].append(c)

    def to_shard(part, b):
        n = far[part][b]
        for c in second_sum[part, b]:
            c.wait_recv()
        if b == 0:
            total = sa[n, h, ch].astype(F32)
            for i in range(NY - 1):
                total = total + qa[n, i].astype(F32)
        else:
            total = sb[n - ni, x].astype(F32)
            for i in range(NX - 1):
                total = total + qb[n - ni, i].astype(F32)
        fb[n] = total.astype(BF16)
        goal = core * half + n * NH + h
        step = (z + nz - goal) % nz

        @pl.when(step != 0)
        def _():
            remote(fb.at[n], zb.at[step], z_send.at[n], z_recv.at[0], (me, goal)).start()

        @pl.when(step == 0)
        def _():
            zb[0] = fb[n]

    for b in range(2):
        to_second(0, b)

    @pl.when(is_src)
    def _():
        wcopy.wait()

    w_small, w_large = {}, {}
    for part in range(ni):
        for b in range(2):
            n = near[part][b]
            line = wf.at[n, h, ch, xrows(x)]

            @pl.when(jnp.logical_not(jnp.logical_and(is_src, own_n == n)))
            def _():
                remote(line, line, wz_send.at[0], wz_recv.at[n], (me, (z + 1) % nz)).wait_recv()

            w_small[part, b] = []
            for s in around((NY, NX)[b]):
                i = s - 1
                if b == 0:
                    to, src = at(x, (y + s) % NY), (y + NY - s) % NY
                    dst = wf.at[n, src // 2, src % 2, xrows(x)]
                else:
                    to, src = at((x + s) % NX, y), (x + NX - s) % NX
                    dst = wf.at[n, h, ch, xrows(src)]
                c = remote(line, line, ws_send.at[n, i], ws_recv.at[n, i], to)
                c.start()
                r = remote(dst, dst, ws_send.at[n, i], ws_recv.at[n, i], to)
                w_small[part, b].append((c, r))

    for part in range(1, ni):
        for b in range(2):
            to_second(part, b)
    for b in range(2):
        to_shard(0, b)

    def line_of(b, n, step, side=None):
        place = on_line(b, step)[0]
        if b == 0:
            return wf.at[n, :, :, xrows(place)] if side is None else wf.at[n, :, side, xrows(place)]
        if side is None:
            return wf.at[n, place // 2, place % 2]
        return wf.at[n, place // 2, place % 2, pl.ds(side * (shard // 2), shard // 2)]

    def w_copy(n, b, i, src, dst, step):
        send, recv, to = wl_send.at[n, i], wl_recv.at[n, i], on_line(b, step)[1]
        return remote(src, src, send, recv, to), remote(dst, dst, send, recv, to)

    for part in range(ni):
        for b in range(2):
            n = near[part][b]
            for c, r in w_small[part, b]:
                r.wait_recv()
            w_large[part, b] = [w_copy(n, b, 0, line_of(b, n, 0), line_of(b, n, -1), 1)]
            if (NX, NY)[b] == 4:
                w_large[part, b].append(w_copy(n, b, 1, line_of(b, n, 0), line_of(b, n, 1), -1))
            for c, r in w_large[part, b]:
                c.start()

    for part in range(1, ni):
        for b in range(2):
            to_shard(part, b)

    rank = rank_ref[...]
    dx = (lax.shift_right_logical(rank, (NY * CORES).bit_length() - 1) - x) & (NX - 1)
    dy = (lax.shift_right_logical(rank, CORES.bit_length() - 1) - y) & (NY - 1)
    rel = (dx * NY + dy) * CORES + ((rank - core) & (CORES - 1))
    target = jnp.where(live, rel.astype(F32) * MAXLEN + slot, -1.0).astype(jnp.int32)
    n_slots = ndp * MAXLEN
    s1h[...] = jnp.where(
        lax.broadcasted_iota(jnp.int32, (n_slots, own), 0) == target, 1.0, 0.0
    ).astype(BF16)
    first = jnp.where(jnp.logical_and(live, slot == 0), rel, -1)
    pack = pack_ref[...].astype(F32)
    hit = lax.broadcasted_iota(jnp.int32, (ndp, 8, own), 0) == first[None]
    begin = jnp.sum(jnp.where(hit, pack[None], 0.0), axis=2, keepdims=True)
    ps[...] = jnp.broadcast_to(begin, (ndp, 8, LANES))
    pr[0] = ps[0]

    def send_begin(s, device):
        remote(ps.at[s], pr.at[s], ps_sem.at[0], ps_sem.at[1], device).start()

    to_peers(send_begin)

    w_relay = {}
    for part in range(ni):
        for b in range(2):
            n = near[part][b]
            w_relay[part, b] = []
            for c, r in w_large[part, b]:
                r.wait_recv()
            if (NX, NY)[b] == 4:
                w_relay[part, b] = [
                    w_copy(n, b, 2, line_of(b, n, -1, 0), line_of(b, n, -2, 0), 1),
                    w_copy(n, b, 3, line_of(b, n, 1, 1), line_of(b, n, 2, 1), -1),
                ]
            for c, r in w_relay[part, b]:
                c.start()

    lane = lax.broadcasted_iota(jnp.int32, (own, LANES), 1)
    for head in range(8 * KV_HEADS):
        side = head // 8 % 2
        tile = uv[:, head // 2 * LANES : (head // 2 + 1) * LANES].astype(F32)
        if head % 2 != side:
            tile = pltpu.roll(tile, HEAD_DIM, 1)
        ub[head] = jnp.where(lane // HEAD_DIM == side, tile, 0.0).astype(BF16)

    x_sib.wait_recv()

    def values_of(n, rows):
        weights = jnp.concatenate([wf[n, :, c].reshape(chunk, LANES) for c in range(2)], axis=1)
        return jnp.dot(rows, weights, preferred_element_type=F32)

    def value_part(i, who):
        total = vp[who] if i > 0 else None
        for n in near[i]:
            if who == 1:
                rows = xs[:, pl.ds(pl.multiple_of(n * chunk, LANES), chunk)]
            else:
                rows = xv[:, pl.ds(pl.multiple_of(core * width + n * chunk, LANES), chunk)]
            part = values_of(n, rows)
            total = part if total is None else total + part
        vp[who] = total

    vp_copy = remote(vp.at[1], vp_sib, vp_sem.at[0], vp_sem.at[1], (sib, z))
    for i in range(ni):
        for b in range(2):
            for c, r in w_relay[i, b]:
                r.wait_recv()
        value_part(i, 1)
        if i == ni - 1:
            vp_copy.start()
        value_part(i, 0)

    def piece_copy(dx, dy, do):
        place = ((x + dx) % NX * NY + (y + dy) % NY) * CORES + ch

        @pl.when(place != me)
        def _():
            do(remote(gs, gb.at[ch, x], g_send.at[dx * NY + dy], g_recv.at[x], (place, z)))

    vp_copy.wait_recv()
    kv[...] = (vp[0] + vp_sib[...]).astype(BF16)

    @pl.when(is_src)
    def _():
        rest = zb.at[1:nz]
        remote(rest, rest, z_send.at[0], z_recv.at[0], (me, (z + 1) % nz)).wait_recv()
        whole = zb[0].astype(F32)
        for i in range(1, nz):
            whole = whole + zb[i].astype(F32)
        gs[...] = whole.astype(BF16)

        @pl.when(ch == core)
        def _():
            gb[ch, x] = whole.astype(BF16)

        for dx in around(NX) + [0]:
            for dy in around(NY) + [0]:
                piece_copy(dx, dy, lambda c: c.start())

    def backward(g):
        pair_lanes = slice(g // 2 * LANES, (g // 2 + 1) * LANES)
        for b, (t0, k0, nk) in enumerate(BLOCKS):
            vals = kv[k0 : k0 + nk, pair_lanes]
            scale = frow[b] * HEAD_DIM**-0.5
            parts = []
            for part in range(2):
                heads = ub[8 * g + 4 * part : 8 * g + 4 * part + 4, t0 : t0 + LANES, :]
                d = lax.dot_general(
                    vals, heads.reshape(4 * LANES, LANES), NT, preferred_element_type=F32
                )
                for r in range(4):
                    head = d[:, r * LANES : (r + 1) * LANES]
                    soft = (p0, p1)[b][g * 2 + part, r]
                    delta = jnp.sum(soft * head, axis=0, keepdims=True)
                    parts.append((soft * (head - delta) * scale).astype(BF16))
            tiles = [
                qv[t0 : t0 + LANES, g * 512 + i * LANES : g * 512 + (i + 1) * LANES]
                for i in range(4)
            ]
            put_rows(acc, g, b, head_sum(parts, tiles, nk))

    for pair in range(2):
        backward(2 * pair)
        backward(2 * pair + 1)
        rows = jnp.dot(s1h[...], join_pair(acc, pair), preferred_element_type=F32)
        ks[:, :, pair * LANES : (pair + 1) * LANES] = rows.astype(BF16).reshape(
            ndp, MAXLEN, LANES
        )
    kr[0] = ks[0]

    def send_rows(s, device):
        remote(ks.at[s], kr.at[s], kk_sem.at[0], kk_sem.at[1], device).start()

    to_peers(send_rows)

    remote(ps.at[1:ndp], pr.at[1:ndp], ps_sem.at[0], ps_sem.at[1], (sib, z)).wait()
    begin = jnp.concatenate([pr[...], pr[...]], axis=1)
    place = begin + lax.broadcasted_iota(jnp.int32, begin.shape, 1).astype(F32)
    lane = lax.broadcasted_iota(jnp.int32, begin.shape, 2).astype(F32)
    put[...] = jnp.where(place == lane, 1.0, 0.0).astype(BF16).reshape(n_slots, LANES)

    for xx in range(NX):
        is_mine = jnp.logical_and(x == xx, ch == core)

        @pl.when(jnp.logical_not(jnp.logical_and(is_src, is_mine)))
        def _():
            dst = gb.at[core, xx]
            remote(dst, dst, g_send.at[0], g_recv.at[xx], (sib, z)).wait_recv()

    g_copy = remote(gb.at[core], gb.at[core], gf_sem.at[0], gf_sem.at[1], (sib, z))
    g_copy.start()
    g_copy.wait_recv()
    for xx in range(NX):
        for c in range(2):
            wgv[xx * piece : (xx + 1) * piece, c * LANES : (c + 1) * LANES] = gb[c, xx].astype(F32)
    wg_copy = pltpu.make_async_copy(wgv, wg_ref, loc.at[0])
    wg_copy.start()

    remote(ks.at[1:ndp], kr.at[1:ndp], kk_sem.at[0], kk_sem.at[1], (sib, z)).wait()
    kgv[...] = lax.dot_general(
        put[...], kr[...].reshape(n_slots, 2 * LANES), TN, preferred_element_type=F32
    ).astype(BF16)
    kg_copy = pltpu.make_async_copy(kgv, kg_ref, loc.at[1])
    kg_copy.start()

    x_sib.wait_send()
    vp_copy.wait_send()
    g_copy.wait_send()
    for n in range(n_all):
        exchange(n).wait_send()
        goal = core * half + n * NH + h

        @pl.when(goal != z)
        def _():
            remote(fb.at[n], zb.at[1], z_send.at[n], z_recv.at[0], (me, goal)).wait_send()

    for part in range(ni):
        for b in range(2):
            for c, r in w_small[part, b] + w_large[part, b] + w_relay[part, b]:
                c.wait_send()
            for c in first_relay[part, b] + first_sum[part, b] + second_sum[part, b]:
                c.wait_send()

    @pl.when(is_src)
    def _():
        def sent_weight(s, carry):
            dst = wf.at[own_n, h, ch, xrows(x)]
            remote(
                w_piece, dst, wz_send.at[s - 1], wz_recv.at[own_n], (me, (z + s) % nz)
            ).wait_send()
            return carry

        lax.fori_loop(1, nz, sent_weight, 0)

        for dx in range(NX):
            for dy in range(NY):
                piece_copy(dx, dy, lambda c: c.wait_send())

    wg_copy.wait()
    kg_copy.wait()


def on_device(
    layer_input,
    queries,
    key_states,
    upstream,
    advantage,
    value_weight,
    row_sample,
    row_rank,
    row_pack,
):
    nz = lax.axis_size("fsdp")
    ndp = NX * NY * CORES
    own, depth = layer_input.shape
    shard, kv_width = value_weight.shape
    piece = shard // NX
    width = depth // 2
    n_all = nz // 2 // NH
    ni = n_all // 2
    vmem = pltpu.VMEM
    dma = pltpu.SemaphoreType.DMA
    hbm = pl.BlockSpec(memory_space=pl.ANY)
    far = max(NX, NY) - 1
    kept = [nk for _, _, nk in BLOCKS]
    return pl.pallas_call(
        functools.partial(kernel, nz),
        out_shape=(
            jax.ShapeDtypeStruct((BAL, kv_width), BF16),
            jax.ShapeDtypeStruct((shard, kv_width), F32),
        ),
        in_specs=[hbm] * 9,
        out_specs=(hbm, hbm),
        scratch_shapes=[
            vmem(queries.shape, BF16),
            vmem(upstream.shape, BF16),
            vmem((own, kv_width), BF16),
            vmem((own, depth), BF16),
            vmem((own, width), BF16),
            vmem((1, own), F32),
            vmem((1, own), jnp.int32),
            vmem((1, own), jnp.int32),
            vmem((1, own), jnp.int32),
            vmem((n_all, NH, 2, shard, LANES), BF16),
            vmem((KV_HEADS, 4, own, 256), BF16),
            vmem((8, 4, kept[0], LANES), F32),
            vmem((8, 4, kept[1], LANES), F32),
            vmem((kept[0], LANES), F32),
            vmem((kept[1], LANES), F32),
            vmem((2, 1, LANES), F32),
            vmem((KV_HEADS, own, LANES), F32),
            vmem((own, kv_width), BF16),
            vmem((n_all, NH, 2, shard, LANES), F32),
            vmem((n_all, NH, 2, shard, LANES), BF16),
            vmem((n_all, NH, 2, shard, LANES), BF16),
            vmem((n_all, NH, 2, shard, LANES), BF16),
            vmem((ni, 2, NH, 2, piece, LANES), BF16),
            vmem((ni, 2, 2, shard // 2, LANES), BF16),
            vmem((ni, 2, NH, piece, LANES), BF16),
            vmem((ni, 2, shard // 2, LANES), BF16),
            vmem((ni, 2, NH, piece, LANES), BF16),
            vmem((ni, 2, shard // 2, LANES), BF16),
            vmem((ni, NH, 2, piece, LANES), BF16),
            vmem((ni, NX, piece, LANES), BF16),
            vmem((ni, NY - 1, piece, LANES), BF16),
            vmem((ni, NX - 1, piece, LANES), BF16),
            vmem((n_all, piece, LANES), BF16),
            vmem((nz, piece, LANES), BF16),
            vmem((2, NX, piece, LANES), BF16),
            vmem((piece, LANES), BF16),
            vmem((shard, kv_width), F32),
            vmem((BAL, kv_width), BF16),
            vmem((2, own, kv_width), F32),
            vmem((own, kv_width), F32),
            vmem((ndp * MAXLEN, own), BF16),
            vmem((ndp, MAXLEN, kv_width), BF16),
            vmem((ndp, MAXLEN, kv_width), BF16),
            vmem((ndp, 8, LANES), F32),
            vmem((ndp, 8, LANES), F32),
            vmem((ndp * MAXLEN, LANES), BF16),
            vmem((8 * KV_HEADS, own, LANES), BF16),
            dma((10,)),
            dma((8,)),
            dma((2,)),
            dma((2, n_all)),
            dma((2,)),
            dma((nz - 1,)),
            dma((n_all,)),
            dma((n_all, far)),
            dma((n_all, far)),
            dma((n_all, 4)),
            dma((n_all, 4)),
            dma((n_all, 6)),
            dma((n_all, 6)),
            dma((n_all, far)),
            dma((n_all, far)),
            dma((n_all,)),
            dma((1,)),
            dma((NX * NY,)),
            dma((NX,)),
            dma((2,)),
            dma((2,)),
            dma((2,)),
        ],
        compiler_params=pltpu.CompilerParams(
            collective_id=0, has_side_effects=True, vmem_limit_bytes=62 * 1024 * 1024
        ),
    )(
        layer_input,
        queries,
        key_states,
        upstream,
        value_weight,
        advantage.reshape(1, own),
        row_sample.reshape(1, own),
        row_rank.reshape(1, own),
        row_pack.reshape(1, own),
    )


def solution(mesh):
    return jax.shard_map(
        on_device,
        mesh=mesh,
        in_specs=(
            P(("dp", "fsdp"), None),
            P(("dp", "fsdp"), None),
            P(("dp", "fsdp"), None),
            P(("dp", "fsdp"), None),
            P(("dp", "fsdp")),
            P("fsdp", None),
            P(("dp", "fsdp")),
            P(("dp", "fsdp")),
            P(("dp", "fsdp")),
        ),
        out_specs=(P(("dp", "fsdp"), None), P("fsdp", None)),
        check_vma=False,
    )
```
